128 devices in a mesh: phase: 2 (over z_hi), seq: 32 (over y, x, core), dp: 2 (over z_lo).
Axes of the slice: x: 4, y: 4, z: 4 (z_hi: 2, z_lo: 2; z = z_hi * 2 + z_lo), core: 2. Of those that a mesh axis runs over, the one named last changes fastest.
Arguments:
- bin_activations: bfloat16 [4, 8192, 768], P('dp', 'seq'), may hold values from -6 to 6
- spaced_filter_coefs: bfloat16 [3, 768, 768], replicated, may hold values from -0.125 to 0.125
- merged_bin_projector: bfloat16 [768, 1536], replicated, may hold values from -0.21875 to 0.21875
- backbone_rms_gain: float32 [1536], replicated, may hold values from 0.5 to 1.5
- asking_projector: bfloat16 [1536, 1024], replicated, may hold values from -0.15625 to 0.15625
- common_lookup_projector: bfloat16 [1536, 256], replicated, may hold values from -0.15625 to 0.15625
- attention_exit_projector: bfloat16 [1024, 1536], replicated, may hold values from -0.1875 to 0.1875
- lane_logit_factor: float32 [8], replicated, may hold values from 1 to 40
- splice_readout_lines: bfloat16 [2, 4, 4096, 1536], P('phase', 'dp', 'seq'), may hold values from -6 to 6
- couple_embedding_cotangent: bfloat16 [2, 4, 4096, 768], P('phase', 'dp', 'seq'), may hold values from -6 to 6
- splice_site_projector: bfloat16 [2, 1536, 768], replicated, may hold values from -0.21875 to 0.21875
- site_locator_code: int32 [2, 4, 32, 32, 16], P('phase', 'dp', 'seq'), may hold values from 0 to 255
- site_local_line: int32 [2, 4, 32, 32, 16], P('phase', 'dp', 'seq'), may hold values from 0 to 127
- filled_slot_totals: int32 [2, 4, 32, 32], P('phase', 'dp', 'seq'), may hold values from 1 to 16, as said below
Outputs:
- phase_rows: bfloat16 [2, 4, 4096, 1536], P('phase', 'dp', 'seq')
- row_grad: bfloat16 [2, 4, 4096, 1536], P('phase', 'dp', 'seq')
- weight_grad: float32 [2, 2, 1536, 768], P('phase', None, ('seq', 'dp'))
The draws below stay inside these ranges and needn't reach their ends.
Inputs may be any that keep to these rules, and one draw needn't show every extreme that they name: `filled_slot_totals`: in each micro-batch and sequence, one receiving shard gets 16 valid slots from every listing shard; the other blocks hold 1 to 8.
All inputs are finite; a program needn't handle non-finite values.
Results may differ from the reference program's by a relative error of at most 0.034.
Values may be sent and summed in bfloat16 or wider, within the bound.
No kernel may reach another device: no remote copies, remote signals or barrier semaphores. Data moves between devices by JAX's collectives and lax.ppermute only.
A program may use at most 128 MiB of HBM per device.

```python
import math
import jax
import jax.numpy as jnp
from jax import lax

C1 = 768
D = 1536
HEADS = 8
ATTN_LANE_SIZE = 128
P_SIZE = 768
KERNEL_TAPS = 3
DILATION_STEP = 2
ROWS_DEV = 128
JUNC_DEV = 128
SLOTS = 16
PHASES = 2
SHARDS = 32
BATCH = 4
ROWS = 4096
CELL_POSITIONS = 8192
JUNCS = 4096


def draw_lane_logit_factor(key, part):
    key = jax.random.fold_in(key, 11)
    logs = jax.random.uniform(key, (HEADS,), jnp.float32, jnp.log(1.0), jnp.log(10.0))
    return jnp.exp(logs)


def draw_filled_slot_totals(key, part):
    key = jax.random.fold_in(key, 7)
    first, second = jax.random.split(key)
    base = jax.random.randint(first, (PHASES, BATCH, SHARDS, SHARDS), 1, SLOTS // 2 + 1)
    busiest = jax.random.randint(second, (PHASES, BATCH, 1, 1), 0, SHARDS)
    target = jnp.arange(SHARDS, dtype=jnp.int32)[None, None, None, :]
    return jnp.where(target == busiest, SLOTS, base).astype(jnp.int32)


def place_ends(entries, key, low, largest):
    extent = entries.shape
    spot = [jax.random.randint(jax.random.fold_in(key, axis), (), 0, extent[axis]) for axis in range(len(extent))]
    entries = entries.at[tuple(spot)].set(low)
    longest = extent.index(max(extent))
    spot[longest] = (spot[longest] + 1) % extent[longest]
    return entries.at[tuple(spot)].set(largest)


def shard_levels(rng, shape, pieces, low, top_value):
    loudness, own = 1.0, jax.random.fold_in(rng, 6)
    for dim, shards_of in pieces:
        draws = jnp.exp(jax.random.uniform(jax.random.fold_in(own, dim), (shards_of,), jnp.float32, low / len(pieces), top_value / len(pieces)))
        loudness = loudness * jnp.repeat(draws, shape[dim] // shards_of).reshape([-1 if axis == dim else 1 for axis in range(len(shape))])
    return loudness


def centred(own_key, dims, width, bound, cuts=(), kind=jnp.bfloat16):
    gain = shard_levels(own_key, dims, cuts, -0.22, 0.18) if cuts else 1.0
    entries = jax.random.normal(own_key, dims, jnp.float32) * width * gain
    return jnp.minimum(jnp.maximum(entries, -bound), bound).astype(kind)


def setup_inputs(seed: int = 0) -> dict:
    key_of = jax.random.split(jax.random.key(seed), 15)
    return {
        "bin_activations": centred(key_of[0], (BATCH, CELL_POSITIONS, C1), 1.0, 6.0, ((0, 2), (1, 32))),
        "spaced_filter_coefs": centred(key_of[1], (KERNEL_TAPS, C1, C1), (KERNEL_TAPS * C1) ** -0.5, 0.125),
        "merged_bin_projector": centred(key_of[2], (C1, D), C1 ** -0.5, 0.21875),
        "backbone_rms_gain": jnp.clip(1.0 + 0.1 * jax.random.normal(key_of[3], (D,), jnp.float32), 0.5, 1.5),
        "asking_projector": centred(key_of[4], (D, HEADS * ATTN_LANE_SIZE), D ** -0.5, 0.15625),
        "common_lookup_projector": centred(key_of[5], (D, 2 * ATTN_LANE_SIZE), D ** -0.5, 0.15625),
        "attention_exit_projector": centred(key_of[6], (HEADS * ATTN_LANE_SIZE, D), (HEADS * ATTN_LANE_SIZE) ** -0.5, 0.1875),
        "lane_logit_factor": draw_lane_logit_factor(jax.random.fold_in(key_of[14], 71), 0),
        "splice_readout_lines": centred(key_of[8], (PHASES, BATCH, ROWS, D), 1.0, 6.0, ((0, 2), (1, 2), (2, 32))),
        "couple_embedding_cotangent": centred(key_of[9], (PHASES, BATCH, JUNCS, P_SIZE), 1.0, 6.0, ((0, 2), (1, 2), (2, 32))),
        "splice_site_projector": centred(key_of[10], (2, D, P_SIZE), P_SIZE ** -0.5, 0.21875),
        "site_locator_code": place_ends(jax.random.randint(key_of[11], (PHASES, BATCH, SHARDS, SHARDS, SLOTS), 0, 2 * JUNC_DEV), jax.random.fold_in(key_of[11], 1), 0, (2 * JUNC_DEV) - 1).astype(jnp.int32),
        "site_local_line": place_ends(jax.random.randint(key_of[12], (PHASES, BATCH, SHARDS, SHARDS, SLOTS), 0, ROWS_DEV), jax.random.fold_in(key_of[12], 1), 0, ROWS_DEV - 1).astype(jnp.int32),
        "filled_slot_totals": draw_filled_slot_totals(jax.random.fold_in(key_of[14], 71), 0),
    }


def encode(seq, spaced_filter_coefs, merged_bin_projector):
    receptive_extent = DILATION_STEP * (KERNEL_TAPS // 2)
    padded_input = jnp.pad(seq, ((receptive_extent, receptive_extent), (0, 0)))
    running_sum = jnp.zeros((CELL_POSITIONS, C1), jnp.float32)
    for kernel_tap in range(KERNEL_TAPS):
        running_sum = running_sum + jnp.dot(padded_input[kernel_tap * DILATION_STEP:kernel_tap * DILATION_STEP + CELL_POSITIONS], spaced_filter_coefs[kernel_tap], preferred_element_type=jnp.float32)
    hidden = seq.astype(jnp.float32) + jax.nn.gelu(running_sum)
    pooled = hidden.reshape(CELL_POSITIONS // 2, 2, C1).mean(axis=1).astype(jnp.bfloat16)
    return jnp.dot(pooled, merged_bin_projector, preferred_element_type=jnp.float32).astype(jnp.bfloat16)

def backbone_block(embedded_bins, backbone_rms_gain, asking_projector, common_lookup_projector, attention_exit_projector, lane_logit_factor):
    wide = embedded_bins.astype(jnp.float32)
    normed = (wide * lax.rsqrt(lax.optimization_barrier(jnp.mean(wide * wide, axis=-1, keepdims=True)) + 1e-06) * backbone_rms_gain).astype(jnp.bfloat16)
    queries = jnp.dot(normed, asking_projector, preferred_element_type=jnp.float32).astype(jnp.bfloat16)
    keyvals = jnp.dot(normed, common_lookup_projector, preferred_element_type=jnp.float32).astype(jnp.bfloat16)
    keys = keyvals[:, :ATTN_LANE_SIZE].astype(jnp.float32)
    values = keyvals[:, ATTN_LANE_SIZE:].astype(jnp.float32)
    logit_multiplier = lane_logit_factor / math.sqrt(ATTN_LANE_SIZE)
    block = math.gcd(ROWS, 512)
    query_blocks = queries.reshape(ROWS // block, block, HEADS, ATTN_LANE_SIZE)

    def attend(query):
        scores = jnp.einsum('qhe,ke->hqk', query.astype(jnp.float32), keys) * logit_multiplier[:, None, None]
        top = lax.optimization_barrier(jnp.max(scores, axis=-1, keepdims=True))
        expo = jnp.exp(scores - top)
        weights = (expo / lax.optimization_barrier(jnp.sum(expo, axis=-1, keepdims=True))).astype(jnp.bfloat16)
        mixed = jnp.einsum('hqk,ke->qhe', weights.astype(jnp.float32), values).astype(jnp.bfloat16)
        return mixed.reshape(block, HEADS * ATTN_LANE_SIZE)
    attended = lax.map(attend, query_blocks).reshape(ROWS, HEADS * ATTN_LANE_SIZE)
    return (wide + jnp.dot(attended, attention_exit_projector, preferred_element_type=jnp.float32)).astype(jnp.bfloat16)

def junction(cotangent, ids, rows, counts, head, splice_site_projector):
    source = jnp.arange(SHARDS, dtype=jnp.int32)[None, :, None, None]
    target_shard = jnp.arange(SHARDS, dtype=jnp.int32)[None, None, :, None]
    slot = jnp.arange(SLOTS, dtype=jnp.int32)[None, None, None, :]
    valid = slot < counts[..., None]
    which = source * JUNC_DEV + ids % JUNC_DEV
    target = ids // JUNC_DEV * ROWS + target_shard * ROWS_DEV + rows

    def collect(cot, whi, tar, val):
        picked = jnp.take(cot.astype(jnp.float32), whi.reshape(-1), axis=0)
        picked = jnp.where(val.reshape(-1, 1), picked, jnp.zeros_like(picked))
        return jax.ops.segment_sum(picked, tar.reshape(-1), num_segments=2 * ROWS)
    summed = jax.vmap(collect)(cotangent, which, target, valid)
    ends = summed.astype(jnp.bfloat16).reshape(BATCH, 2, ROWS, P_SIZE).astype(jnp.float32)
    grads = jnp.einsum('bkrp,kdp->brd', ends, splice_site_projector.astype(jnp.float32)).astype(jnp.bfloat16)
    weight = jnp.einsum('brd,bkrp->kdp', head.astype(jnp.float32), ends)
    return (grads, weight)

def reference(bin_activations, spaced_filter_coefs, merged_bin_projector, backbone_rms_gain, asking_projector, common_lookup_projector, attention_exit_projector, lane_logit_factor, splice_readout_lines, couple_embedding_cotangent, splice_site_projector, site_locator_code, site_local_line, filled_slot_totals):
    embedded_bins = lax.map(lambda seq: encode(seq, spaced_filter_coefs, merged_bin_projector), bin_activations)
    backbone_result = lax.map(lambda sequence_reader_memory: backbone_block(sequence_reader_memory, backbone_rms_gain, asking_projector, common_lookup_projector, attention_exit_projector, lane_logit_factor), embedded_bins)
    phase_rows = jnp.stack([embedded_bins, backbone_result])
    grads = []
    weights = []
    for micro in range(PHASES):
        grad, weight = junction(couple_embedding_cotangent[micro], site_locator_code[micro], site_local_line[micro], filled_slot_totals[micro], splice_readout_lines[micro], splice_site_projector)
        grads.append(grad)
        weights.append(weight)
    return (phase_rows, jnp.stack(grads), jnp.stack(weights))
```

```python
import math

import jax
import jax.numpy as jnp
from jax import lax
from jax.sharding import Mesh
from jax.sharding import PartitionSpec as P

DILATION_STEP = 2
SEQ = ("y", "x", "core")
F32 = jnp.float32
BF16 = jnp.bfloat16


def dot(a, b, dims=(((1,), (0,)), ((), ()))):
    return lax.dot_general(a, b, dims, preferred_element_type=F32)


def halo(block, width):
    count = lax.axis_size(SEQ)
    forward = [(i, i + 1) for i in range(count - 1)]
    backward = [(b, a) for a, b in forward]
    low = lax.ppermute(block[:, -width:], SEQ, forward)
    high = lax.ppermute(block[:, :width], SEQ, backward)
    return jnp.concatenate([low, block, high], axis=1)


def body(
    bin_activations,
    spaced_filter_coefs,
    merged_bin_projector,
    backbone_rms_gain,
    asking_projector,
    common_lookup_projector,
    attention_exit_projector,
    lane_logit_factor,
    splice_readout_lines,
    couple_embedding_cotangent,
    splice_site_projector,
    site_locator_code,
    site_local_line,
    filled_slot_totals,
):
    phase = lax.axis_index("phase")
    core = lax.axis_index("core")
    batch, cells, chans = bin_activations.shape
    rows = cells // 2
    width = merged_bin_projector.shape[1]
    taps = spaced_filter_coefs.shape[0]
    extent = DILATION_STEP * (taps // 2)
    heads = lane_logit_factor.shape[0]
    lane = common_lookup_projector.shape[1] // 2
    swap = [(0, 1), (1, 0)]

    cotangent = couple_embedding_cotangent[0]
    junc = cotangent.shape[1]
    embed = cotangent.shape[2]
    ids = site_locator_code[0, :, 0]
    lines = site_local_line[0, :, 0]
    counts = filled_slot_totals[0, :, 0]
    shards, slots = ids.shape[1:]
    valid = lax.broadcasted_iota(jnp.int32, ids.shape, 2) < counts[..., None]
    codes = jnp.where(valid, ids // junc * rows + lines, -1)
    which = jnp.where(valid, ids % junc, -1)
    pick = (
        which.reshape(batch, shards * slots, 1) == jnp.arange(junc, dtype=jnp.int32)
    ).astype(BF16)
    picked = dot(pick, cotangent, (((2,), (1,)), ((0,), (0,)))).astype(BF16)
    tags = jnp.broadcast_to(
        codes.astype(BF16).reshape(batch, shards * slots, 1), (batch, shards * slots, 128)
    )
    payload = jnp.concatenate([picked, tags], axis=-1)
    payload = payload.reshape(batch, shards, slots, embed + 128).transpose(1, 0, 2, 3)
    arrived = lax.all_to_all(payload, SEQ, 0, 0, tiled=True)

    padded_input = halo(bin_activations, extent)
    total = jnp.zeros((batch, cells, chans), F32)
    for tap in range(taps):
        total = total + jnp.einsum(
            "bpc,cd->bpd",
            padded_input[:, tap * DILATION_STEP : tap * DILATION_STEP + cells],
            spaced_filter_coefs[tap],
            preferred_element_type=F32,
        )
    hidden = bin_activations.astype(F32) + jax.nn.gelu(total)
    pooled = hidden.reshape(batch, rows, 2, chans).mean(axis=2).astype(BF16)
    encoded = jnp.einsum(
        "brc,cd->brd", pooled, merged_bin_projector, preferred_element_type=F32
    ).astype(BF16)

    wide = encoded.astype(F32)
    normed = (
        wide
        * lax.rsqrt(jnp.mean(wide * wide, axis=-1, keepdims=True) + 1e-06)
        * backbone_rms_gain
    ).astype(BF16)
    keyvals = jnp.einsum(
        "brd,de->bre", normed, common_lookup_projector, preferred_element_type=F32
    ).astype(BF16)
    gathered = lax.all_gather(keyvals, SEQ, axis=1, tiled=True)
    queries = jnp.einsum(
        "brd,de->bre", normed, asking_projector, preferred_element_type=F32
    ).astype(BF16)

    portion = splice_readout_lines[0].reshape(batch * rows, width)
    blocks = shards // 2
    lines_t = portion.T.reshape(blocks, 2, width // (2 * blocks), batch * rows)
    mine = lax.dynamic_index_in_dim(lines_t, core, 1, keepdims=False)
    other = lax.dynamic_index_in_dim(lines_t, 1 - core, 1, keepdims=False)
    other = lax.ppermute(other, "core", swap)
    lines_t = jnp.concatenate([mine, other], axis=2).reshape(width // 2, 2 * batch * rows)

    data = arrived[..., :embed].transpose(1, 0, 2, 3).reshape(batch, shards * slots, embed)
    tag = arrived[..., embed:].transpose(1, 0, 2, 3).reshape(batch, shards * slots, 128)
    ends = []
    for kind in range(2):
        target = (jnp.arange(rows, dtype=jnp.int32) + kind * rows).astype(BF16)
        onehot = (tag[:, :, :rows] == target).astype(BF16)
        ends.append(dot(onehot, data, (((1,), (1,)), ((0,), (0,)))).astype(BF16))
    ends = jnp.concatenate(ends, axis=-1).reshape(batch * rows, 2 * embed)
    ends_other = lax.ppermute(ends, "core", swap)
    partial = dot(lines_t, jnp.concatenate([ends, ends_other], axis=0)).astype(BF16)
    partial = partial.reshape(shards, width // (2 * shards), 2 * embed)
    pieces = lax.all_to_all(partial, ("y", "x", "dp"), 0, 0, tiled=True)

    row_grad = (
        dot(ends[:, :embed], splice_site_projector[0], (((1,), (1,)), ((), ())))
        + dot(ends[:, embed:], splice_site_projector[1], (((1,), (1,)), ((), ())))
    ).astype(BF16)
    row_grad = row_grad.reshape(batch, rows, width)[None]

    logit = lane_logit_factor / math.sqrt(lane)

    def attend_one(operands):
        query, keyval = operands
        query = query.reshape(rows, heads, lane)
        scores = (
            jnp.einsum("qhe,ke->hqk", query, keyval[:, :lane], preferred_element_type=F32)
            * logit[:, None, None]
        )
        top = jnp.max(scores, axis=-1, keepdims=True)
        expo = jnp.exp(scores - top)
        weights = (expo / jnp.sum(expo, axis=-1, keepdims=True)).astype(BF16)
        mixed = jnp.einsum(
            "hqk,ke->qhe", weights, keyval[:, lane:], preferred_element_type=F32
        ).astype(BF16)
        return mixed.reshape(rows, heads * lane)

    def trunk():
        attended = lax.map(attend_one, (queries, gathered))
        mixed = jnp.einsum(
            "brh,hd->brd", attended, attention_exit_projector, preferred_element_type=F32
        )
        return (encoded.astype(F32) + mixed).astype(BF16)

    phase_rows = lax.cond(phase == 1, trunk, lambda: encoded)[None]

    summed = jnp.sum(pieces.astype(F32), axis=0)
    weight_grad = summed.reshape(-1, 2, embed).transpose(1, 0, 2)[None]
    return (phase_rows, row_grad, weight_grad)


def solution(mesh):
    shape = dict(mesh.shape)
    side = math.isqrt(shape["seq"] // 2)
    fine = Mesh(
        mesh.devices.reshape(shape["phase"], side, side, 2, shape["dp"]),
        ("phase", "y", "x", "core", "dp"),
    )
    return jax.shard_map(
        body,
        mesh=fine,
        in_specs=(
            P("dp", SEQ, None),
            P(),
            P(),
            P(),
            P(),
            P(),
            P(),
            P(),
            P("phase", "dp", SEQ, None),
            P("phase", "dp", SEQ, None),
            P(),
            P("phase", "dp", SEQ, None, None),
            P("phase", "dp", SEQ, None, None),
            P("phase", "dp", SEQ, None),
        ),
        out_specs=(
            P("phase", "dp", SEQ, None),
            P("phase", "dp", SEQ, None),
            P("phase", None, SEQ + ("dp",), None),
        ),
        check_vma=False,
    )
```

```python
import functools
import math

import jax
import jax.numpy as jnp
from jax import lax
from jax.experimental import pallas as pl
from jax.experimental.pallas import tpu as pltpu
from jax.sharding import Mesh
from jax.sharding import PartitionSpec as P

DILATION_STEP = 2
SEQ = ("y", "x", "core")
F32 = jnp.float32
BF16 = jnp.bfloat16
I32 = jnp.int32
TAG = 128
NT = (((1,), (1,)), ((), ()))
TN = (((0,), (0,)), ((), ()))
VMEM = pl.BlockSpec(memory_space=pltpu.VMEM)
SMEM = pl.BlockSpec(memory_space=pltpu.SMEM)
ANY = pl.BlockSpec(memory_space=pl.ANY)


def dot(a, b, dims=(((1,), (0,)), ((), ()))):
    return lax.dot_general(a, b, dims, preferred_element_type=F32)


def params(mib):
    return pltpu.CompilerParams(vmem_limit_bytes=mib << 20)


def cost(flops, nbytes):
    return pl.CostEstimate(flops=int(flops), bytes_accessed=int(nbytes), transcendentals=0)


def pick_kernel(ids_ref, lines_ref, counts_ref, cot_ref, out_ref):
    batch, shards, slots = ids_ref.shape
    junc, embed = cot_ref.shape[1:]
    n = shards * slots
    owner = lax.broadcasted_iota(I32, (n, shards), 0) // slots
    spread = owner == lax.broadcasted_iota(I32, (n, shards), 1)
    spread16 = spread.astype(F32).astype(BF16)
    slot = lax.broadcasted_iota(I32, (n, slots), 0) % slots
    own = slot == lax.broadcasted_iota(I32, (n, slots), 1)

    def column(values):
        wide = dot(spread16, values.astype(F32).astype(BF16))
        return jnp.sum(jnp.where(own, wide, 0.0), axis=1, keepdims=True)

    for b in range(batch):
        ids = ids_ref[b]
        junction = column(ids % junc)
        code = column(ids // junc) * float(junc) + column(lines_ref[b])
        count = jnp.sum(
            jnp.where(spread, counts_ref[b : b + 1, :].astype(F32), 0.0), axis=1, keepdims=True
        )
        valid = slot[:, :1].astype(F32) < count
        junction = jnp.where(valid, junction, -1.0).astype(I32)
        code = jnp.where(valid, code, -1.0)
        onehot = (junction == lax.broadcasted_iota(I32, (n, junc), 1)).astype(F32).astype(BF16)
        picked = dot(onehot, cot_ref[b]).astype(BF16)
        out_ref[:, b, :, :embed] = picked.reshape(shards, slots, embed)
        tags = jnp.broadcast_to(code, (n, TAG)).astype(BF16)
        out_ref[:, b, :, embed:] = tags.reshape(shards, slots, TAG)


def pick(ids, lines, counts, cotangent):
    batch, shards, slots = ids.shape
    embed = cotangent.shape[2]
    return pl.pallas_call(
        pick_kernel,
        out_shape=jax.ShapeDtypeStruct((shards, batch, slots, embed + TAG), BF16),
        in_specs=[VMEM] * 4,
        out_specs=VMEM,
        compiler_params=params(32),
        cost_estimate=cost(2 * 10**8, 3 * 10**6),
        name="pick",
    )(ids, lines, counts, cotangent)


def ends_kernel(arrived_ref, out_ref):
    shards, batch, slots, wide = arrived_ref.shape
    embed = wide - TAG
    n = shards * slots
    rows = out_ref.shape[0] // batch
    for b in range(batch):
        data = arrived_ref[:, b, :, :embed].reshape(n, embed)
        tag = arrived_ref[:, b, :, embed:].reshape(n, TAG).astype(F32)
        for kind in range(2):
            target = lax.broadcasted_iota(I32, (n, rows), 1) + kind * rows
            onehot = (tag == target.astype(F32)).astype(F32).astype(BF16)
            out_ref[b * rows : (b + 1) * rows, kind * embed : (kind + 1) * embed] = dot(
                onehot, data, TN
            ).astype(BF16)


def make_ends(arrived, rows):
    batch, embed = arrived.shape[1], arrived.shape[3] - TAG
    return pl.pallas_call(
        ends_kernel,
        out_shape=jax.ShapeDtypeStruct((batch * rows, 2 * embed), BF16),
        in_specs=[VMEM],
        out_specs=VMEM,
        compiler_params=params(32),
        cost_estimate=cost(4 * 10**8, 3 * 10**6),
        name="ends",
    )(arrived)


def turn_kernel(core_ref, lines_ref, mine_ref, other_ref):
    blocks, part, n = mine_ref.shape
    first = core_ref[0] == 0
    turned = lines_ref[...].T.reshape(blocks, 2, part, n)
    low, high = turned[:, 0], turned[:, 1]
    mine_ref[...] = jnp.where(first, low, high)
    other_ref[...] = jnp.where(first, high, low)


def turn(core, lines, blocks):
    n, width = lines.shape
    half = jax.ShapeDtypeStruct((blocks, width // (2 * blocks), n), BF16)
    return pl.pallas_call(
        turn_kernel,
        out_shape=(half, half),
        in_specs=[SMEM, VMEM],
        out_specs=(VMEM, VMEM),
        compiler_params=params(32),
        cost_estimate=cost(10**6, 2 * 10**6),
        name="turn",
    )(core.reshape(1), lines)


def partial_kernel(mine_ref, other_ref, ends_ref, ends_other_ref, out_ref):
    rows, n = mine_ref.shape[0] * mine_ref.shape[1], mine_ref.shape[2]
    total = dot(mine_ref[...].reshape(rows, n), ends_ref[...])
    total = total + dot(other_ref[...].reshape(rows, n), ends_other_ref[...])
    out_ref[...] = total.astype(BF16).reshape(out_ref.shape)


def partial_grad(mine, other, ends, ends_other, pieces):
    rows, width = mine.shape[0] * mine.shape[1], ends.shape[1]
    return pl.pallas_call(
        partial_kernel,
        out_shape=jax.ShapeDtypeStruct((pieces, rows // pieces, width), BF16),
        in_specs=[VMEM] * 4,
        out_specs=VMEM,
        compiler_params=params(40),
        cost_estimate=cost(1.2 * 10**9, 5 * 10**6),
        name="partial_grad",
    )(mine, other, ends, ends_other)


def encoder_kernel(
    x_ref,
    low_ref,
    high_ref,
    gain_ref,
    taps_hbm,
    merge_hbm,
    look_hbm,
    ask_hbm,
    rows_ref,
    query_ref,
    keyval_ref,
    taps,
    merge,
    look,
    ask,
    pad,
    hidden,
    sems,
):
    copies = [
        pltpu.make_async_copy(source, target, sems.at[i])
        for i, (source, target) in enumerate(
            ((taps_hbm, taps), (merge_hbm, merge), (look_hbm, look), (ask_hbm, ask))
        )
    ]
    for copy in copies:
        copy.start()
    batch, cells, chans = x_ref.shape
    extent = low_ref.shape[1]
    base = 8
    for b in range(batch):
        pad[b, base - extent : base, :] = low_ref[b].astype(F32)
        pad[b, base : base + cells, :] = x_ref[b].astype(F32)
        pad[b, base + cells : base + cells + extent, :] = high_ref[b].astype(F32)
    copies[0].wait()
    for b in range(batch):
        total = dot(x_ref[b], taps[1])
        total += dot(pad[b, base - extent : base - extent + cells, :].astype(BF16), taps[0])
        total += dot(pad[b, base + extent : base + extent + cells, :].astype(BF16), taps[2])
        total = pad[b, base : base + cells, :] + jax.nn.gelu(total)
        for j in range(hidden.shape[0]):
            hidden[j, b * cells : (b + 1) * cells, :] = total[:, j * 128 : (j + 1) * 128]
    n = batch * cells // 2
    pooled = jnp.concatenate(
        [
            ((hidden[j, pl.ds(0, n, 2), :] + hidden[j, pl.ds(1, n, 2), :]) * 0.5).astype(BF16)
            for j in range(hidden.shape[0])
        ],
        axis=1,
    )
    copies[1].wait()
    rows = dot(pooled, merge[...]).astype(BF16)
    rows_ref[...] = rows
    wide = rows.astype(F32)
    scale = lax.rsqrt(jnp.mean(wide * wide, axis=-1, keepdims=True) + 1e-06)
    normed = (wide * scale * gain_ref[...]).astype(BF16)
    copies[2].wait()
    keyval_ref[...] = dot(normed, look[...]).astype(BF16)
    copies[3].wait()
    query_ref[...] = dot(normed, ask[...]).astype(BF16)


def encode(x, low, high, gain, taps, merge, look, ask):
    batch, cells, chans = x.shape
    n = batch * cells // 2
    width = merge.shape[1]
    return pl.pallas_call(
        encoder_kernel,
        out_shape=(
            jax.ShapeDtypeStruct((n, width), BF16),
            jax.ShapeDtypeStruct((n, ask.shape[1]), BF16),
            jax.ShapeDtypeStruct((n, look.shape[1]), BF16),
        ),
        in_specs=[VMEM] * 4 + [ANY] * 4,
        out_specs=(VMEM,) * 3,
        scratch_shapes=[
            pltpu.VMEM(taps.shape, BF16),
            pltpu.VMEM(merge.shape, BF16),
            pltpu.VMEM(look.shape, BF16),
            pltpu.VMEM(ask.shape, BF16),
            pltpu.VMEM((batch, cells + 16, chans), F32),
            pltpu.VMEM((chans // 128, batch * cells, 128), F32),
            pltpu.SemaphoreType.DMA((4,)),
        ],
        compiler_params=params(48),
        cost_estimate=cost(3.4 * 10**9, 12 * 10**6),
        name="encode",
    )(x, low, high, gain.reshape(1, width), taps, merge, look, ask)


def trunk_kernel(
    phase_ref, logit_ref, query_ref, keyval_ref, rows_ref, exit_ref, out_ref, attended
):
    b, pair = pl.program_id(0), pl.program_id(1)
    pairs = pl.num_programs(1)
    lane = keyval_ref.shape[2] // 2
    rows = query_ref.shape[0]
    last = jnp.logical_and(b == pl.num_programs(0) - 1, pair == pairs - 1)
    on = phase_ref[0] == 1

    @pl.when(on)
    def _():
        query = jnp.concatenate([query_ref[:, :lane], query_ref[:, lane:]], axis=0)
        scores = dot(query, keyval_ref[0, :, :lane], NT)
        upper = lax.broadcasted_iota(I32, (2 * rows, 1), 0) < rows
        factor = jnp.where(upper, logit_ref[2 * pair], logit_ref[2 * pair + 1])
        top = jnp.max(scores, axis=-1, keepdims=True)
        expo = jnp.exp2(scores * factor - top * factor)
        total = jnp.sum(expo, axis=-1, keepdims=True)
        mixed = dot(expo.astype(BF16), keyval_ref[0, :, lane:])
        mixed = (mixed / total).astype(BF16)
        attended[pair, pl.ds(pl.multiple_of(b * rows, rows), rows), :lane] = mixed[:rows]
        attended[pair, pl.ds(pl.multiple_of(b * rows, rows), rows), lane:] = mixed[rows:]

    @pl.when(jnp.logical_and(on, last))
    def _():
        out = rows_ref[...].astype(F32)
        for i in range(attended.shape[0]):
            out += dot(attended[i], exit_ref[2 * i * lane : 2 * (i + 1) * lane, :])
        out_ref[...] = out.astype(BF16)

    @pl.when(jnp.logical_and(jnp.logical_not(on), last))
    def _():
        out_ref[...] = rows_ref[...]


def trunk(phase, logit, queries, gathered, encoded, exit_projector):
    batch, keys, both = gathered.shape
    n, width = encoded.shape
    rows = n // batch
    pairs = queries.shape[1] // both
    return pl.pallas_call(
        trunk_kernel,
        grid=(batch, pairs),
        out_shape=jax.ShapeDtypeStruct((n, width), BF16),
        in_specs=[
            SMEM,
            SMEM,
            pl.BlockSpec((rows, both), lambda b, p: (b, p)),
            pl.BlockSpec((1, keys, both), lambda b, p: (b, 0, 0)),
            pl.BlockSpec((n, width), lambda b, p: (0, 0)),
            pl.BlockSpec(exit_projector.shape, lambda b, p: (0, 0)),
        ],
        out_specs=pl.BlockSpec((n, width), lambda b, p: (0, 0)),
        scratch_shapes=[pltpu.VMEM((pairs, n, both), BF16)],
        compiler_params=params(56),
        cost_estimate=cost(5.2 * 10**9, 9 * 10**6),
        name="trunk",
    )(phase.reshape(1), logit, queries, gathered, encoded, exit_projector)


def halo(block, width):
    count = lax.axis_size(SEQ)
    forward = [(i, i + 1) for i in range(count - 1)]
    backward = [(b, a) for a, b in forward]
    low = lax.ppermute(block[:, -width:], SEQ, forward)
    high = lax.ppermute(block[:, :width], SEQ, backward)
    return low, high


def body(
    bin_activations,
    spaced_filter_coefs,
    merged_bin_projector,
    backbone_rms_gain,
    asking_projector,
    common_lookup_projector,
    attention_exit_projector,
    lane_logit_factor,
    splice_readout_lines,
    couple_embedding_cotangent,
    splice_site_projector,
    site_locator_code,
    site_local_line,
    filled_slot_totals,
):
    phase = lax.axis_index("phase")
    core = lax.axis_index("core")
    batch, cells, chans = bin_activations.shape
    rows = cells // 2
    width = merged_bin_projector.shape[1]
    extent = DILATION_STEP * (spaced_filter_coefs.shape[0] // 2)
    lane = common_lookup_projector.shape[1] // 2
    embed = couple_embedding_cotangent.shape[3]
    shards = site_locator_code.shape[3]
    swap = [(0, 1), (1, 0)]

    low, high = halo(bin_activations, extent)
    payload = pick(
        site_locator_code[0, :, 0],
        site_local_line[0, :, 0],
        filled_slot_totals[0, :, 0],
        couple_embedding_cotangent[0],
    )
    arrived = lax.all_to_all(payload, SEQ, 0, 0, tiled=True)

    encoded, queries, keyvals = encode(
        bin_activations,
        low,
        high,
        backbone_rms_gain,
        spaced_filter_coefs,
        merged_bin_projector,
        common_lookup_projector,
        asking_projector,
    )
    gathered = lax.all_gather(keyvals.reshape(batch, rows, 2 * lane), SEQ, axis=1, tiled=True)

    portion = splice_readout_lines[0].reshape(batch * rows, width)
    mine, other = turn(core, portion, shards // 2)
    other = lax.ppermute(other, "core", swap)

    ends = make_ends(arrived, rows)
    ends_other = lax.ppermute(ends, "core", swap)
    partial = partial_grad(mine, other, ends, ends_other, shards)
    pieces = lax.all_to_all(partial, ("y", "x", "dp"), 0, 0, tiled=True)

    row_grad = (
        dot(ends[:, :embed], splice_site_projector[0], NT)
        + dot(ends[:, embed:], splice_site_projector[1], NT)
    ).astype(BF16)
    row_grad = row_grad.reshape(batch, rows, width)[None]

    logit = lane_logit_factor * (math.log2(math.e) / math.sqrt(lane))
    phase_rows = trunk(phase, logit, queries, gathered, encoded, attention_exit_projector)
    phase_rows = phase_rows.reshape(batch, rows, width)[None]

    summed = jnp.sum(pieces.astype(F32), axis=0)
    weight_grad = summed.reshape(-1, 2, embed).transpose(1, 0, 2)[None]
    return (phase_rows, row_grad, weight_grad)


def solution(mesh):
    shape = dict(mesh.shape)
    side = math.isqrt(shape["seq"] // 2)
    fine = Mesh(
        mesh.devices.reshape(shape["phase"], side, side, 2, shape["dp"]),
        ("phase", "y", "x", "core", "dp"),
    )
    return jax.shard_map(
        body,
        mesh=fine,
        in_specs=(
            P("dp", SEQ, None),
            P(),
            P(),
            P(),
            P(),
            P(),
            P(),
            P(),
            P("phase", "dp", SEQ, None),
            P("phase", "dp", SEQ, None),
            P(),
            P("phase", "dp", SEQ, None, None),
            P("phase", "dp", SEQ, None, None),
            P("phase", "dp", SEQ, None),
        ),
        out_specs=(
            P("phase", "dp", SEQ, None),
            P("phase", "dp", SEQ, None),
            P("phase", None, SEQ + ("dp",), None),
        ),
        check_vma=False,
    )
```

```python
import functools
import math

import jax
import jax.numpy as jnp
from jax import lax
from jax.experimental import pallas as pl
from jax.experimental.pallas import tpu as pltpu
from jax.sharding import Mesh
from jax.sharding import PartitionSpec as P

DILATION_STEP = 2
SEQ = ("y", "x", "core")
F32 = jnp.float32
BF16 = jnp.bfloat16
I32 = jnp.int32
TAG = 128
NT = (((1,), (1,)), ((), ()))
TN = (((0,), (0,)), ((), ()))
VMEM = pl.BlockSpec(memory_space=pltpu.VMEM)
SMEM = pl.BlockSpec(memory_space=pltpu.SMEM)
ANY = pl.BlockSpec(memory_space=pl.ANY)
HBM = pl.BlockSpec(memory_space=pltpu.HBM)


def dot(a, b, dims=(((1,), (0,)), ((), ()))):
    return lax.dot_general(a, b, dims, preferred_element_type=F32)


def params(mib):
    return pltpu.CompilerParams(vmem_limit_bytes=mib << 20)


TOKEN = jax.ShapeDtypeStruct((8, 128), F32)


def cost(flops, nbytes):
    return pl.CostEstimate(flops=int(flops), bytes_accessed=int(nbytes), transcendentals=0)


def pick_kernel(
    ids_hbm,
    lines_hbm,
    counts_hbm,
    cot_hbm,
    _low,
    _high,
    out_ref,
    token_ref,
    ids_ref,
    lines_ref,
    counts_ref,
    cot_ref,
    sems,
):
    pairs = ((ids_hbm, ids_ref), (lines_hbm, lines_ref), (counts_hbm, counts_ref), (cot_hbm, cot_ref))
    copies = [
        pltpu.make_async_copy(source, target, sems.at[i])
        for i, (source, target) in enumerate(pairs)
    ]
    for copy in copies:
        copy.start()
    token_ref[...] = jnp.zeros_like(token_ref)
    batch, slots, shards = ids_ref.shape
    junc, embed = cot_ref.shape[1:]
    n = shards * slots
    owner = lax.broadcasted_iota(I32, (n, shards), 0) // slots
    spread = owner == lax.broadcasted_iota(I32, (n, shards), 1)
    spread16 = spread.astype(F32).astype(BF16)
    slot = lax.broadcasted_iota(I32, (n, slots), 0) % slots
    own = slot == lax.broadcasted_iota(I32, (n, slots), 1)

    def column(values):
        wide = dot(spread16, values.astype(F32).astype(BF16), NT)
        return jnp.sum(jnp.where(own, wide, 0.0), axis=1, keepdims=True)

    for copy in copies:
        copy.wait()
    for b in range(batch):
        ids = ids_ref[b]
        junction = column(ids % junc)
        code = column(ids // junc) * float(junc) + column(lines_ref[b])
        count = jnp.sum(
            jnp.where(spread, counts_ref[b : b + 1, :].astype(F32), 0.0), axis=1, keepdims=True
        )
        valid = slot[:, :1].astype(F32) < count
        junction = jnp.where(valid, junction, -1.0).astype(I32)
        code = jnp.where(valid, code, -1.0)
        onehot = (junction == lax.broadcasted_iota(I32, (n, junc), 1)).astype(F32).astype(BF16)
        picked = dot(onehot, cot_ref[b]).astype(BF16)
        out_ref[:, b, :, :embed] = picked.reshape(shards, slots, embed)
        tags = jnp.broadcast_to(code, (n, TAG)).astype(BF16)
        out_ref[:, b, :, embed:] = tags.reshape(shards, slots, TAG)


def pick(ids, lines, counts, cotangent, low, high):
    batch, slots, shards = ids.shape
    embed = cotangent.shape[2]
    return pl.pallas_call(
        pick_kernel,
        out_shape=(
            jax.ShapeDtypeStruct((shards, batch, slots, embed + TAG), BF16),
            TOKEN,
        ),
        in_specs=[ANY] * 6,
        out_specs=(VMEM, VMEM),
        scratch_shapes=[
            pltpu.VMEM(ids.shape, I32),
            pltpu.VMEM(lines.shape, I32),
            pltpu.VMEM(counts.shape, I32),
            pltpu.VMEM(cotangent.shape, BF16),
            pltpu.SemaphoreType.DMA((4,)),
        ],
        compiler_params=params(56),
        cost_estimate=cost(2 * 10**8, 3 * 10**6),
        name="pick",
    )(ids, lines, counts, cotangent, low, high)


def ends_kernel(arrived_ref, _, out_ref):
    shards, batch, slots, wide = arrived_ref.shape
    embed = wide - TAG
    n = shards * slots
    rows = out_ref.shape[0] // batch
    for b in range(batch):
        data = arrived_ref[:, b, :, :embed].reshape(n, embed)
        tag = arrived_ref[:, b, :, embed:].reshape(n, TAG).astype(F32)
        for kind in range(2):
            target = lax.broadcasted_iota(I32, (n, rows), 1) + kind * rows
            onehot = (tag == target.astype(F32)).astype(F32).astype(BF16)
            out_ref[b * rows : (b + 1) * rows, kind * embed : (kind + 1) * embed] = dot(
                onehot, data, TN
            ).astype(BF16)


def make_ends(arrived, rows, after):
    batch, embed = arrived.shape[1], arrived.shape[3] - TAG
    return pl.pallas_call(
        ends_kernel,
        out_shape=jax.ShapeDtypeStruct((batch * rows, 2 * embed), BF16),
        in_specs=[VMEM, ANY],
        out_specs=VMEM,
        compiler_params=params(32),
        cost_estimate=cost(4 * 10**8, 3 * 10**6),
        name="ends",
    )(arrived, after)


def turn_kernel(core_ref, lines_ref, mine_ref, other_ref):
    blocks, part, n = mine_ref.shape
    first = core_ref[0] == 0
    turned = lines_ref[...].T.reshape(blocks, 2, part, n)
    low, high = turned[:, 0], turned[:, 1]
    mine_ref[...] = jnp.where(first, low, high)
    other_ref[...] = jnp.where(first, high, low)


def turn(core, lines, blocks):
    n, width = lines.shape
    half = jax.ShapeDtypeStruct((blocks, width // (2 * blocks), n), BF16)
    return pl.pallas_call(
        turn_kernel,
        out_shape=(half, half),
        in_specs=[SMEM, VMEM],
        out_specs=(VMEM, VMEM),
        compiler_params=params(32),
        cost_estimate=cost(10**6, 2 * 10**6),
        name="turn",
    )(core.reshape(1), lines)


def partial_kernel(mine_ref, other_ref, ends_ref, ends_other_ref, out_ref, token_ref):
    token_ref[...] = jnp.zeros_like(token_ref)
    rows, n = mine_ref.shape[0] * mine_ref.shape[1], mine_ref.shape[2]
    total = dot(mine_ref[...].reshape(rows, n), ends_ref[...])
    total = total + dot(other_ref[...].reshape(rows, n), ends_other_ref[...])
    out_ref[...] = total.astype(BF16).reshape(out_ref.shape)


def partial_grad(mine, other, ends, ends_other, pieces):
    rows, width = mine.shape[0] * mine.shape[1], ends.shape[1]
    return pl.pallas_call(
        partial_kernel,
        out_shape=(jax.ShapeDtypeStruct((pieces, rows // pieces, width), BF16), TOKEN),
        in_specs=[VMEM] * 4,
        out_specs=(VMEM, VMEM),
        compiler_params=params(40),
        cost_estimate=cost(1.2 * 10**9, 5 * 10**6),
        name="partial_grad",
    )(mine, other, ends, ends_other)


def encoder_kernel(
    core_ref,
    low_ref,
    high_ref,
    gain_ref,
    x_hbm,
    taps_hbm,
    merge_hbm,
    look_hbm,
    ask_hbm,
    after_ref,
    rows_hbm,
    key_own_ref,
    key_out_ref,
    query_own_ref,
    query_out_ref,
    token_ref,
    x_ref,
    taps,
    merge,
    look,
    ask,
    pad,
    hidden,
    rows_ref,
    sems,
):
    pairs = ((x_hbm, x_ref), (taps_hbm, taps), (merge_hbm, merge), (look_hbm, look), (ask_hbm, ask))
    copies = [
        pltpu.make_async_copy(source, target, sems.at[i])
        for i, (source, target) in enumerate(pairs)
    ]
    for copy in copies:
        copy.start()
    out_copy = pltpu.make_async_copy(rows_ref, rows_hbm, sems.at[len(pairs)])
    batch, cells, chans = x_ref.shape
    extent = low_ref.shape[1]
    base = 8
    copies[0].wait()
    for b in range(batch):
        pad[b, base - extent : base, :] = low_ref[b].astype(F32)
        pad[b, base : base + cells, :] = x_ref[b].astype(F32)
        pad[b, base + cells : base + cells + extent, :] = high_ref[b].astype(F32)
    copies[1].wait()
    for b in range(batch):
        total = dot(x_ref[b], taps[1])
        total += dot(pad[b, base - extent : base - extent + cells, :].astype(BF16), taps[0])
        total += dot(pad[b, base + extent : base + extent + cells, :].astype(BF16), taps[2])
        total = pad[b, base : base + cells, :] + jax.nn.gelu(total)
        for j in range(hidden.shape[0]):
            hidden[j, b * cells : (b + 1) * cells, :] = total[:, j * 128 : (j + 1) * 128]
    n = batch * cells // 2
    pooled = jnp.concatenate(
        [
            ((hidden[j, pl.ds(0, n, 2), :] + hidden[j, pl.ds(1, n, 2), :]) * 0.5).astype(BF16)
            for j in range(hidden.shape[0])
        ],
        axis=1,
    )
    copies[2].wait()
    rows = dot(pooled, merge[...]).astype(BF16)
    rows_ref[...] = rows
    out_copy.start()
    wide = rows.astype(F32)
    scale = lax.rsqrt(jnp.mean(wide * wide, axis=-1, keepdims=True) + 1e-06)
    normed = (wide * scale * gain_ref[...]).astype(BF16)
    half = n // 2
    first = core_ref[0] == 0

    def halves(value, own_ref, out_ref):
        own_ref[...] = jnp.where(first, value[:half], value[half:])
        out_ref[...] = jnp.where(first, value[half:], value[:half])

    copies[3].wait()
    halves(dot(normed, look[...]).astype(BF16), key_own_ref, key_out_ref)
    copies[4].wait()
    halves(dot(normed, ask[...]).astype(BF16), query_own_ref, query_out_ref)
    token_ref[...] = jnp.zeros_like(token_ref)
    out_copy.wait()


def encode(core, x, low, high, gain, taps, merge, look, ask, after):
    batch, cells, chans = x.shape
    n = batch * cells // 2
    width = merge.shape[1]
    key = jax.ShapeDtypeStruct((n // 2, look.shape[1]), BF16)
    query = jax.ShapeDtypeStruct((n // 2, ask.shape[1]), BF16)
    return pl.pallas_call(
        encoder_kernel,
        out_shape=(jax.ShapeDtypeStruct((n, width), BF16), key, key, query, query, TOKEN),
        in_specs=[SMEM] + [VMEM] * 3 + [HBM] * 5 + [ANY],
        out_specs=(HBM,) + (VMEM,) * 5,
        scratch_shapes=[
            pltpu.VMEM(x.shape, BF16),
            pltpu.VMEM(taps.shape, BF16),
            pltpu.VMEM(merge.shape, BF16),
            pltpu.VMEM(look.shape, BF16),
            pltpu.VMEM(ask.shape, BF16),
            pltpu.VMEM((batch, cells + 16, chans), F32),
            pltpu.VMEM((chans // 128, batch * cells, 128), F32),
            pltpu.VMEM((n, width), BF16),
            pltpu.SemaphoreType.DMA((6,)),
        ],
        compiler_params=params(56),
        cost_estimate=cost(3.4 * 10**9, 12 * 10**6),
        name="encode",
    )(core.reshape(1), low, high, gain.reshape(1, width), x, taps, merge, look, ask, after)


def attend_kernel(
    phase_ref, logit_ref, query_own_ref, query_in_ref, *refs
):
    keys, (_, own_ref, out_ref) = refs[:-3], refs[-3:]
    rows, width = query_own_ref.shape
    lane = keys[0].shape[1] // 2
    pieces = [key.at[i : i + 512] for key in keys for i in range(0, key.shape[0], 512)]

    def head(h):
        span = pl.ds(pl.multiple_of(h * lane, lane), lane)
        query = jnp.concatenate([query_own_ref[:, span], query_in_ref[:, span]], axis=0)
        factor = logit_ref[h]
        scores = [dot(query, piece[:, :lane], NT) for piece in pieces]
        top = functools.reduce(jnp.maximum, scores)
        top = jnp.max(top, axis=-1, keepdims=True) * factor
        mixed, total = 0.0, 0.0
        for score, piece in zip(scores, pieces):
            expo = jnp.exp2(score * factor - top)
            total = total + expo
            mixed = mixed + dot(expo.astype(BF16), piece[:, lane:])
        total = jnp.sum(total, axis=-1, keepdims=True)
        mixed = (mixed / total).astype(BF16)
        own_ref[:, span] = mixed[:rows]
        out_ref[:, span] = mixed[rows:]

    @pl.when(phase_ref[0] == 1)
    def _():
        @pl.loop(0, width // lane // 2)
        def _(i):
            head(2 * i)
            head(2 * i + 1)


def attend(phase, logit, query_own, query_in, keys, after):
    shape = jax.ShapeDtypeStruct(query_own.shape, BF16)
    return pl.pallas_call(
        attend_kernel,
        out_shape=(shape, shape),
        in_specs=[SMEM, SMEM] + [VMEM] * (2 + len(keys)) + [ANY],
        out_specs=(VMEM, VMEM),
        compiler_params=params(24),
        cost_estimate=cost(6 * 10**10, 4 * 10**6),
        name="attend",
    )(phase.reshape(1), logit, query_own, query_in, *keys, after)


def exit_kernel(phase_ref, core_ref, rows_ref, own_ref, in_ref, exit_ref, out_ref, token_ref):
    token_ref[...] = jnp.zeros_like(token_ref)
    n = own_ref.shape[0]
    on = phase_ref[0] == 1

    @pl.when(on)
    def _():
        attended = jnp.concatenate([own_ref[...], in_ref[...]], axis=0)
        mixed = dot(attended, exit_ref[...])
        for i in range(2):
            owner = core_ref[0] if i == 0 else 1 - core_ref[0]
            span = pl.ds(pl.multiple_of(owner * n, n), n)
            out_ref[span, :] = (rows_ref[span, :].astype(F32) + mixed[i * n : (i + 1) * n]).astype(
                BF16
            )

    @pl.when(jnp.logical_not(on))
    def _():
        out_ref[...] = rows_ref[...]


def leave(phase, core, encoded, own, arrived, exit_projector):
    return pl.pallas_call(
        exit_kernel,
        out_shape=(jax.ShapeDtypeStruct(encoded.shape, BF16), TOKEN),
        in_specs=[SMEM, SMEM] + [VMEM] * 4,
        out_specs=(VMEM, VMEM),
        compiler_params=params(32),
        cost_estimate=cost(8 * 10**8, 5 * 10**6),
        name="leave",
    )(phase.reshape(1), core.reshape(1), encoded, own, arrived, exit_projector)


def gather_terms_kernel(pieces_ref, _, out_ref):
    embed = out_ref.shape[2]
    total = jnp.sum(pieces_ref[...].astype(F32), axis=0)
    for kind in range(2):
        out_ref[kind] = total[:, kind * embed : (kind + 1) * embed]


def sum_terms(pieces, after):
    _, rows, width = pieces.shape
    return pl.pallas_call(
        gather_terms_kernel,
        out_shape=jax.ShapeDtypeStruct((2, rows, width // 2), F32),
        in_specs=[VMEM, ANY],
        out_specs=VMEM,
        compiler_params=params(32),
        cost_estimate=cost(10**6, 3 * 10**6),
        name="sum_terms",
    )(pieces, after)


def stack_kernel(*refs):
    blocks, (out_ref, token_ref) = refs[:-2], refs[-2:]
    rows = blocks[0].shape[0]
    for i, block in enumerate(blocks):
        out_ref[i * rows : (i + 1) * rows, :] = block[...]
    token_ref[...] = jnp.zeros_like(token_ref)


def stack(blocks):
    rows, width = blocks[0].shape
    return pl.pallas_call(
        stack_kernel,
        out_shape=(jax.ShapeDtypeStruct((len(blocks) * rows, width), BF16), TOKEN),
        in_specs=[VMEM] * len(blocks),
        out_specs=(VMEM, VMEM),
        compiler_params=params(8),
        cost_estimate=cost(10**5, 10**6),
        name="stack",
    )(*blocks)


def spread(block, side, first):
    received = []
    for distance in (1, side - 1, 2):
        pairs = []
        for y in range(side):
            for x in range(side):
                for core in range(2):
                    along_x = (core == 0) == first
                    to_x = (x + distance) % side if along_x else x
                    to_y = y if along_x else (y + distance) % side
                    pairs.append(((y * side + x) * 2 + core, (to_y * side + to_x) * 2 + core))
        received.append(lax.ppermute(block, SEQ, pairs))
    return received


def halo(block, width):
    count = lax.axis_size(SEQ)
    forward = [(i, i + 1) for i in range(count - 1)]
    backward = [(b, a) for a, b in forward]
    low = lax.ppermute(block[:, -width:], SEQ, forward)
    high = lax.ppermute(block[:, :width], SEQ, backward)
    return low, high


def body(
    bin_activations,
    spaced_filter_coefs,
    merged_bin_projector,
    backbone_rms_gain,
    asking_projector,
    common_lookup_projector,
    attention_exit_projector,
    lane_logit_factor,
    splice_readout_lines,
    couple_embedding_cotangent,
    splice_site_projector,
    site_locator_code,
    site_local_line,
    filled_slot_totals,
):
    phase = lax.axis_index("phase")
    core = lax.axis_index("core")
    batch, cells, chans = bin_activations.shape
    rows = cells // 2
    width = merged_bin_projector.shape[1]
    extent = DILATION_STEP * (spaced_filter_coefs.shape[0] // 2)
    lane = common_lookup_projector.shape[1] // 2
    embed = couple_embedding_cotangent.shape[3]
    shards = site_locator_code.shape[3]
    swap = [(0, 1), (1, 0)]
    side = lax.axis_size("y")

    low, high = halo(bin_activations, extent)
    payload, picked = pick(
        jnp.swapaxes(site_locator_code[0, :, 0], 1, 2),
        jnp.swapaxes(site_local_line[0, :, 0], 1, 2),
        filled_slot_totals[0, :, 0],
        couple_embedding_cotangent[0],
        low,
        high,
    )
    arrived = lax.all_to_all(payload, SEQ, 0, 0, tiled=True)

    encoded, key_own, key_out, query_own, query_out, _ = encode(
        core,
        bin_activations,
        low,
        high,
        backbone_rms_gain,
        spaced_filter_coefs,
        merged_bin_projector,
        common_lookup_projector,
        asking_projector,
        picked,
    )
    chip_keys, _ = stack([key_own, lax.ppermute(key_out, "core", swap)])
    line_keys, line_done = stack([chip_keys] + spread(chip_keys, side, True))
    keys = [line_keys] + spread(line_keys, side, False)
    query_in = lax.ppermute(query_out, "core", swap)

    portion = splice_readout_lines[0].reshape(batch * rows, width)
    mine, other = turn(core, portion, shards // 2)
    other = lax.ppermute(other, "core", swap)

    ends = make_ends(arrived, rows, line_done)
    ends_other = lax.ppermute(ends, "core", swap)
    partial, terms_done = partial_grad(mine, other, ends, ends_other, shards)
    pieces = lax.all_to_all(partial, ("y", "x", "dp"), 0, 0, tiled=True)

    row_grad = (
        dot(ends[:, :embed], splice_site_projector[0], NT)
        + dot(ends[:, embed:], splice_site_projector[1], NT)
    ).astype(BF16)
    row_grad = row_grad.reshape(batch, rows, width)[None]

    logit = lane_logit_factor * (math.log2(math.e) / math.sqrt(lane))
    own, out = attend(phase, logit, query_own, query_in, keys, terms_done)
    rows_out, left = leave(
        phase, core, encoded, own, lax.ppermute(out, "core", swap), attention_exit_projector
    )
    phase_rows = rows_out.reshape(batch, rows, width)[None]

    weight_grad = sum_terms(pieces, left)[None]
    return (phase_rows, row_grad, weight_grad)


def solution(mesh):
    shape = dict(mesh.shape)
    side = math.isqrt(shape["seq"] // 2)
    fine = Mesh(
        mesh.devices.reshape(shape["phase"], side, side, 2, shape["dp"]),
        ("phase", "y", "x", "core", "dp"),
    )
    return jax.shard_map(
        body,
        mesh=fine,
        in_specs=(
            P("dp", SEQ, None),
            P(),
            P(),
            P(),
            P(),
            P(),
            P(),
            P(),
            P("phase", "dp", SEQ, None),
            P("phase", "dp", SEQ, None),
            P(),
            P("phase", "dp", SEQ, None, None),
            P("phase", "dp", SEQ, None, None),
            P("phase", "dp", SEQ, None),
        ),
        out_specs=(
            P("phase", "dp", SEQ, None),
            P("phase", "dp", SEQ, None),
            P("phase", None, SEQ + ("dp",), None),
        ),
        check_vma=False,
    )
```

```python
import functools
import math

import jax
import jax.numpy as jnp
from jax import lax
from jax.experimental import pallas as pl
from jax.experimental.pallas import tpu as pltpu
from jax.sharding import Mesh
from jax.sharding import PartitionSpec as P

DILATION_STEP = 2
SEQ = ("y", "x", "core")
F32 = jnp.float32
BF16 = jnp.bfloat16
I32 = jnp.int32
TAG = 128
NT = (((1,), (1,)), ((), ()))
TN = (((0,), (0,)), ((), ()))
VMEM = pl.BlockSpec(memory_space=pltpu.VMEM)
SMEM = pl.BlockSpec(memory_space=pltpu.SMEM)
ANY = pl.BlockSpec(memory_space=pl.ANY)
HBM = pl.BlockSpec(memory_space=pltpu.HBM)


def dot(a, b, dims=(((1,), (0,)), ((), ()))):
    return lax.dot_general(a, b, dims, preferred_element_type=F32)


def params(mib):
    return pltpu.CompilerParams(vmem_limit_bytes=mib << 20)


TOKEN = jax.ShapeDtypeStruct((8, 128), F32)


def cost(flops, nbytes):
    return pl.CostEstimate(flops=int(flops), bytes_accessed=int(nbytes), transcendentals=0)


def pick_kernel(
    ids_hbm,
    lines_hbm,
    counts_hbm,
    cot_hbm,
    out_ref,
    token_ref,
    ids_ref,
    lines_ref,
    counts_ref,
    cot_ref,
    sems,
):
    pairs = ((ids_hbm, ids_ref), (lines_hbm, lines_ref), (counts_hbm, counts_ref), (cot_hbm, cot_ref))
    copies = [
        pltpu.make_async_copy(source, target, sems.at[i])
        for i, (source, target) in enumerate(pairs)
    ]
    for copy in copies:
        copy.start()
    token_ref[...] = jnp.zeros_like(token_ref)
    batch, slots, shards = ids_ref.shape
    junc, embed = cot_ref.shape[1:]
    n = shards * slots
    owner = lax.broadcasted_iota(I32, (n, shards), 0) // slots
    spread = owner == lax.broadcasted_iota(I32, (n, shards), 1)
    spread16 = spread.astype(F32).astype(BF16)
    slot = lax.broadcasted_iota(I32, (n, slots), 0) % slots
    own = slot == lax.broadcasted_iota(I32, (n, slots), 1)

    def column(values):
        wide = dot(spread16, values.astype(F32).astype(BF16), NT)
        return jnp.sum(jnp.where(own, wide, 0.0), axis=1, keepdims=True)

    for copy in copies:
        copy.wait()
    tags = []
    for b in range(batch):
        ids = ids_ref[b]
        junction = column(ids % junc)
        code = column(ids // junc) * float(junc) + column(lines_ref[b])
        count = jnp.sum(
            jnp.where(spread, counts_ref[b : b + 1, :].astype(F32), 0.0), axis=1, keepdims=True
        )
        valid = slot[:, :1].astype(F32) < count
        junction = jnp.where(valid, junction, -1.0).astype(I32)
        tags.append(jnp.broadcast_to(jnp.where(valid, code, -1.0), (n, TAG)))
        onehot = (junction == lax.broadcasted_iota(I32, (n, junc), 1)).astype(F32).astype(BF16)
        picked = dot(onehot, cot_ref[b]).astype(BF16)
        out_ref[:, :, b * embed : (b + 1) * embed] = picked.reshape(shards, slots, embed)
    lane = lax.broadcasted_iota(I32, (n, TAG), 1)
    tag = tags[0]
    for b in range(1, batch):
        tag = jnp.where(lane < b * (TAG // batch), tag, tags[b])
    out_ref[:, :, batch * embed :] = tag.astype(BF16).reshape(shards, slots, TAG)


def pick(ids, lines, counts, cotangent):
    batch, slots, shards = ids.shape
    embed = cotangent.shape[2]
    return pl.pallas_call(
        pick_kernel,
        out_shape=(
            jax.ShapeDtypeStruct((shards, slots, batch * embed + TAG), BF16),
            TOKEN,
        ),
        in_specs=[ANY] * 4,
        out_specs=(VMEM, VMEM),
        scratch_shapes=[
            pltpu.VMEM(ids.shape, I32),
            pltpu.VMEM(lines.shape, I32),
            pltpu.VMEM(counts.shape, I32),
            pltpu.VMEM(cotangent.shape, BF16),
            pltpu.SemaphoreType.DMA((4,)),
        ],
        compiler_params=params(56),
        cost_estimate=cost(2 * 10**8, 3 * 10**6),
        name="pick",
    )(ids, lines, counts, cotangent)


def follow(value, *after):
    return pl.pallas_call(
        lambda *refs: None,
        out_shape=jax.ShapeDtypeStruct(value.shape, value.dtype),
        in_specs=[ANY] * (1 + len(after)),
        out_specs=ANY,
        input_output_aliases={0: 0},
        name="follow",
    )(value, *after)


def ends_kernel(arrived_ref, _token, _other, out_ref):
    shards, slots, wide = arrived_ref.shape
    embed = out_ref.shape[1] // 2
    batch = (wide - TAG) // embed
    n = shards * slots
    rows = out_ref.shape[0] // batch
    tags = arrived_ref[:, :, batch * embed :].reshape(n, TAG).astype(F32)
    for b in range(batch):
        data = arrived_ref[:, :, b * embed : (b + 1) * embed].reshape(n, embed)
        lane = b * (TAG // batch)
        tag = jnp.broadcast_to(tags[:, lane : lane + 1], (n, rows))
        for kind in range(2):
            target = lax.broadcasted_iota(I32, (n, rows), 1) + kind * rows
            onehot = (tag == target.astype(F32)).astype(F32).astype(BF16)
            out_ref[b * rows : (b + 1) * rows, kind * embed : (kind + 1) * embed] = dot(
                onehot, data, TN
            ).astype(BF16)


def make_ends(arrived, batch, rows, token, other):
    embed = (arrived.shape[2] - TAG) // batch
    return pl.pallas_call(
        ends_kernel,
        out_shape=jax.ShapeDtypeStruct((batch * rows, 2 * embed), BF16),
        in_specs=[VMEM, ANY, ANY],
        out_specs=VMEM,
        compiler_params=params(24),
        cost_estimate=cost(4 * 10**8, 3 * 10**6),
        name="ends",
    )(arrived, token, other)


def row_grad_kernel(ends_ref, head_ref, _token, out_ref):
    embed = head_ref.shape[2]
    total = dot(ends_ref[:, :embed], head_ref[0], NT)
    total = total + dot(ends_ref[:, embed:], head_ref[1], NT)
    out_ref[...] = total.astype(BF16)


def make_row_grad(ends, head, token):
    n, both = ends.shape
    width, embed = head.shape[1:]
    step = 512
    return pl.pallas_call(
        row_grad_kernel,
        grid=(width // step,),
        out_shape=jax.ShapeDtypeStruct((n, width), BF16),
        in_specs=[
            pl.BlockSpec((n, both), lambda i: (0, 0)),
            pl.BlockSpec((2, step, embed), lambda i: (0, i, 0)),
            ANY,
        ],
        out_specs=pl.BlockSpec((n, step), lambda i: (0, i)),
        compiler_params=params(24),
        cost_estimate=cost(1.2 * 10**9, 6 * 10**6),
        name="row_grad",
    )(ends, head, token)


def turn_kernel(core_ref, lines_ref, mine_ref, other_ref):
    blocks, part, n = mine_ref.shape
    first = core_ref[0] == 0
    turned = lines_ref[...].T.reshape(blocks, 2, part, n)
    low, high = turned[:, 0], turned[:, 1]
    mine_ref[...] = jnp.where(first, low, high)
    other_ref[...] = jnp.where(first, high, low)


def turn(core, lines, blocks):
    n, width = lines.shape
    half = jax.ShapeDtypeStruct((blocks, width // (2 * blocks), n), BF16)
    return pl.pallas_call(
        turn_kernel,
        out_shape=(half, half),
        in_specs=[SMEM, VMEM],
        out_specs=(VMEM, VMEM),
        compiler_params=params(32),
        cost_estimate=cost(10**6, 2 * 10**6),
        name="turn",
    )(core.reshape(1), lines)


def partial_kernel(mine_ref, other_ref, ends_ref, ends_other_ref, out_ref, token_ref):
    token_ref[...] = jnp.zeros_like(token_ref)
    rows, n = mine_ref.shape[0] * mine_ref.shape[1], mine_ref.shape[2]
    total = dot(mine_ref[...].reshape(rows, n), ends_ref[...])
    total = total + dot(other_ref[...].reshape(rows, n), ends_other_ref[...])
    out_ref[...] = total.astype(BF16).reshape(out_ref.shape)


def partial_grad(mine, other, ends, ends_other, pieces):
    rows, width = mine.shape[0] * mine.shape[1], ends.shape[1]
    return pl.pallas_call(
        partial_kernel,
        out_shape=(jax.ShapeDtypeStruct((pieces, rows // pieces, width), BF16), TOKEN),
        in_specs=[VMEM] * 4,
        out_specs=(VMEM, VMEM),
        compiler_params=params(40),
        cost_estimate=cost(1.2 * 10**9, 5 * 10**6),
        name="partial_grad",
    )(mine, other, ends, ends_other)


def encoder_kernel(
    core_ref,
    low_ref,
    high_ref,
    gain_ref,
    x_hbm,
    taps_hbm,
    merge_hbm,
    look_hbm,
    ask_hbm,
    after_ref,
    rows_hbm,
    key_own_ref,
    key_out_ref,
    query_own_ref,
    query_out_ref,
    token_ref,
    x_ref,
    taps,
    merge,
    look,
    ask,
    pad,
    hidden,
    rows_ref,
    sems,
):
    pairs = ((x_hbm, x_ref), (taps_hbm, taps), (merge_hbm, merge), (look_hbm, look), (ask_hbm, ask))
    copies = [
        pltpu.make_async_copy(source, target, sems.at[i])
        for i, (source, target) in enumerate(pairs)
    ]
    for copy in copies:
        copy.start()
    out_copy = pltpu.make_async_copy(rows_ref, rows_hbm, sems.at[len(pairs)])
    batch, cells, chans = x_ref.shape
    extent = low_ref.shape[1]
    base = 8
    copies[0].wait()
    for b in range(batch):
        pad[b, base - extent : base, :] = low_ref[b].astype(F32)
        pad[b, base : base + cells, :] = x_ref[b].astype(F32)
        pad[b, base + cells : base + cells + extent, :] = high_ref[b].astype(F32)
    copies[1].wait()
    for b in range(batch):
        before = pad[b, base - extent : base - extent + cells, :].astype(BF16)
        behind = pad[b, base + extent : base + extent + cells, :].astype(BF16)
        for j in range(0, chans, 256):
            span = slice(j, j + 256)
            total = dot(x_ref[b], taps[1, :, span])
            total += dot(before, taps[0, :, span]) + dot(behind, taps[2, :, span])
            total = pad[b, base : base + cells, span] + jax.nn.gelu(total)
            for i in range(0, 256, 128):
                hidden[(j + i) // 128, b * cells : (b + 1) * cells, :] = total[:, i : i + 128]
    n = batch * cells // 2
    pooled = jnp.concatenate(
        [
            ((hidden[j, pl.ds(0, n, 2), :] + hidden[j, pl.ds(1, n, 2), :]) * 0.5).astype(BF16)
            for j in range(hidden.shape[0])
        ],
        axis=1,
    )
    copies[2].wait()
    rows = dot(pooled, merge[...]).astype(BF16)
    rows_ref[...] = rows
    out_copy.start()
    wide = rows.astype(F32)
    scale = lax.rsqrt(jnp.mean(wide * wide, axis=-1, keepdims=True) + 1e-06)
    normed = (wide * scale * gain_ref[...]).astype(BF16)
    half = n // 2
    first = core_ref[0] == 0

    def halves(value, own_ref, out_ref):
        own_ref[...] = jnp.where(first, value[:half], value[half:])
        out_ref[...] = jnp.where(first, value[half:], value[:half])

    copies[3].wait()
    halves(dot(normed, look[...]).astype(BF16), key_own_ref, key_out_ref)
    copies[4].wait()
    halves(dot(normed, ask[...]).astype(BF16), query_own_ref, query_out_ref)
    token_ref[...] = jnp.zeros_like(token_ref)
    out_copy.wait()


def encode(core, x, low, high, gain, taps, merge, look, ask, after):
    batch, cells, chans = x.shape
    n = batch * cells // 2
    width = merge.shape[1]
    key = jax.ShapeDtypeStruct((n // 2, look.shape[1]), BF16)
    query = jax.ShapeDtypeStruct((n // 2, ask.shape[1]), BF16)
    return pl.pallas_call(
        encoder_kernel,
        out_shape=(jax.ShapeDtypeStruct((n, width), BF16), key, key, query, query, TOKEN),
        in_specs=[SMEM] + [VMEM] * 3 + [HBM] * 5 + [ANY],
        out_specs=(HBM,) + (VMEM,) * 5,
        scratch_shapes=[
            pltpu.VMEM(x.shape, BF16),
            pltpu.VMEM(taps.shape, BF16),
            pltpu.VMEM(merge.shape, BF16),
            pltpu.VMEM(look.shape, BF16),
            pltpu.VMEM(ask.shape, BF16),
            pltpu.VMEM((batch, cells + 16, chans), F32),
            pltpu.VMEM((chans // 128, batch * cells, 128), F32),
            pltpu.VMEM((n, width), BF16),
            pltpu.SemaphoreType.DMA((6,)),
        ],
        compiler_params=params(56),
        cost_estimate=cost(3.4 * 10**9, 12 * 10**6),
        name="encode",
    )(core.reshape(1), low, high, gain.reshape(1, width), x, taps, merge, look, ask, after)


def attend_kernel(phase_ref, logit_ref, query_own_ref, query_in_ref, *refs):
    keys, (_, own_ref, out_ref, key_t, value) = refs[:-5], refs[-5:]
    rows, width = query_own_ref.shape
    n, both = keys[0].shape
    lane = both // 2
    count = n * len(keys)
    chunk = 512

    @pl.when(phase_ref[0] == 1)
    def _():
        for i, block in enumerate(keys):
            span = slice(i * n, (i + 1) * n)
            turned = block[:, :lane].T
            key_t[:lane, span] = turned
            key_t[lane:, span] = turned
            value[span, :lane] = block[:, lane:]
            value[span, lane:] = jnp.ones((n, lane), BF16)
        for head in range(width // lane):
            span = slice(head * lane, (head + 1) * lane)
            query = jnp.concatenate([query_own_ref[:, span], query_in_ref[:, span]], axis=0)
            query = query.astype(F32) * logit_ref[head]
            coarse = query.astype(BF16)
            fine = (query - coarse.astype(F32)).astype(BF16)
            query = jnp.concatenate([coarse, fine], axis=1)
            scores = [dot(query, key_t[:, j : j + chunk]) for j in range(0, count, chunk)]
            top = jnp.max(functools.reduce(jnp.maximum, scores), axis=-1, keepdims=True)
            mixed = 0.0
            for j, score in enumerate(scores):
                weight = jnp.exp2(score - top).astype(BF16)
                mixed = mixed + dot(weight, value[j * chunk : (j + 1) * chunk, :])
            mixed = (mixed[:, :lane] / mixed[:, lane:]).astype(BF16)
            own_ref[:, span] = mixed[:rows]
            out_ref[:, span] = mixed[rows:]


def attend(phase, logit, query_own, query_in, keys, after):
    shape = jax.ShapeDtypeStruct(query_own.shape, BF16)
    n, both = keys[0].shape
    count = n * len(keys)
    return pl.pallas_call(
        attend_kernel,
        out_shape=(shape, shape),
        in_specs=[SMEM, SMEM] + [VMEM] * (2 + len(keys)) + [ANY],
        out_specs=(VMEM, VMEM),
        scratch_shapes=[pltpu.VMEM((both, count), BF16), pltpu.VMEM((count, both), BF16)],
        compiler_params=params(32),
        cost_estimate=cost(6 * 10**10, 4 * 10**6),
        name="attend",
    )(phase.reshape(1), logit, query_own, query_in, *keys, after)


def exit_kernel(phase_ref, core_ref, rows_ref, own_ref, in_ref, exit_ref, out_ref, token_ref):
    token_ref[...] = jnp.zeros_like(token_ref)
    n = own_ref.shape[0]
    on = phase_ref[0] == 1

    @pl.when(on)
    def _():
        attended = jnp.concatenate([own_ref[...], in_ref[...]], axis=0)
        mixed = dot(attended, exit_ref[...])
        for i in range(2):
            owner = core_ref[0] if i == 0 else 1 - core_ref[0]
            span = pl.ds(pl.multiple_of(owner * n, n), n)
            out_ref[span, :] = (rows_ref[span, :].astype(F32) + mixed[i * n : (i + 1) * n]).astype(
                BF16
            )

    @pl.when(jnp.logical_not(on))
    def _():
        out_ref[...] = rows_ref[...]


def leave(phase, core, encoded, own, arrived, exit_projector):
    return pl.pallas_call(
        exit_kernel,
        out_shape=(jax.ShapeDtypeStruct(encoded.shape, BF16), TOKEN),
        in_specs=[SMEM, SMEM] + [VMEM] * 4,
        out_specs=(VMEM, VMEM),
        compiler_params=params(32),
        cost_estimate=cost(8 * 10**8, 5 * 10**6),
        name="leave",
    )(phase.reshape(1), core.reshape(1), encoded, own, arrived, exit_projector)


def gather_terms_kernel(pieces_ref, _, out_ref):
    embed = out_ref.shape[2]
    total = jnp.sum(pieces_ref[...].astype(F32), axis=0)
    for kind in range(2):
        out_ref[kind] = total[:, kind * embed : (kind + 1) * embed]


def sum_terms(pieces, after):
    _, rows, width = pieces.shape
    return pl.pallas_call(
        gather_terms_kernel,
        out_shape=jax.ShapeDtypeStruct((2, rows, width // 2), F32),
        in_specs=[VMEM, ANY],
        out_specs=VMEM,
        compiler_params=params(32),
        cost_estimate=cost(10**6, 3 * 10**6),
        name="sum_terms",
    )(pieces, after)


def stack_kernel(*refs):
    blocks, (out_ref, token_ref) = refs[:-2], refs[-2:]
    rows = blocks[0].shape[0]
    for i, block in enumerate(blocks):
        out_ref[i * rows : (i + 1) * rows, :] = block[...]
    token_ref[...] = jnp.zeros_like(token_ref)


def stack(blocks):
    rows, width = blocks[0].shape
    return pl.pallas_call(
        stack_kernel,
        out_shape=(jax.ShapeDtypeStruct((len(blocks) * rows, width), BF16), TOKEN),
        in_specs=[VMEM] * len(blocks),
        out_specs=(VMEM, VMEM),
        compiler_params=params(8),
        cost_estimate=cost(10**5, 10**6),
        name="stack",
    )(*blocks)


def spread(block, side, first):
    received = []
    for distance in (1, side - 1, 2):
        pairs = []
        for y in range(side):
            for x in range(side):
                for core in range(2):
                    along_x = (core == 0) == first
                    to_x = (x + distance) % side if along_x else x
                    to_y = y if along_x else (y + distance) % side
                    pairs.append(((y * side + x) * 2 + core, (to_y * side + to_x) * 2 + core))
        received.append(lax.ppermute(block, SEQ, pairs))
    return received


def halo(first, last):
    count = lax.axis_size(SEQ)
    forward = [(i, i + 1) for i in range(count - 1)]
    backward = [(b, a) for a, b in forward]
    return lax.ppermute(last, SEQ, forward), lax.ppermute(first, SEQ, backward)


def body(
    bin_activations,
    spaced_filter_coefs,
    merged_bin_projector,
    backbone_rms_gain,
    asking_projector,
    common_lookup_projector,
    attention_exit_projector,
    lane_logit_factor,
    splice_readout_lines,
    couple_embedding_cotangent,
    splice_site_projector,
    site_locator_code,
    site_local_line,
    filled_slot_totals,
):
    phase = lax.axis_index("phase")
    core = lax.axis_index("core")
    batch, cells, chans = bin_activations.shape
    rows = cells // 2
    width = merged_bin_projector.shape[1]
    extent = DILATION_STEP * (spaced_filter_coefs.shape[0] // 2)
    lane = common_lookup_projector.shape[1] // 2
    shards = site_locator_code.shape[3]
    swap = [(0, 1), (1, 0)]
    side = lax.axis_size("y")

    first, last = bin_activations[:, :extent], bin_activations[:, -extent:]
    low, high = halo(first, last)
    payload, picked = pick(
        jnp.swapaxes(site_locator_code[0, :, 0], 1, 2),
        jnp.swapaxes(site_local_line[0, :, 0], 1, 2),
        filled_slot_totals[0, :, 0],
        couple_embedding_cotangent[0],
    )
    payload = follow(payload, low, high)
    arrived = lax.all_to_all(payload, SEQ, 0, 0, tiled=True)

    encoded, key_own, key_out, query_own, query_out, _ = encode(
        core,
        bin_activations,
        low,
        high,
        backbone_rms_gain,
        spaced_filter_coefs,
        merged_bin_projector,
        common_lookup_projector,
        asking_projector,
        picked,
    )
    chip_keys, _ = stack([key_own, lax.ppermute(key_out, "core", swap)])
    line_keys, line_done = stack([chip_keys] + spread(chip_keys, side, True))
    keys = [line_keys] + spread(line_keys, side, False)
    query_in = lax.ppermute(query_out, "core", swap)

    portion = splice_readout_lines[0].reshape(batch * rows, width)
    mine, other = turn(core, portion, shards // 2)
    other = lax.ppermute(other, "core", swap)

    ends = make_ends(arrived, batch, rows, line_done, other)
    ends_other = lax.ppermute(ends, "core", swap)
    partial, terms_done = partial_grad(mine, other, ends, ends_other, shards)
    pieces = lax.all_to_all(partial, ("y", "x", "dp"), 0, 0, tiled=True)

    row_grad = make_row_grad(ends, splice_site_projector, terms_done)
    row_grad = row_grad.reshape(batch, rows, width)[None]

    logit = lane_logit_factor * (math.log2(math.e) / math.sqrt(lane))
    own, out = attend(phase, logit, query_own, query_in, keys, terms_done)
    rows_out, left = leave(
        phase, core, encoded, own, lax.ppermute(out, "core", swap), attention_exit_projector
    )
    phase_rows = rows_out.reshape(batch, rows, width)[None]

    weight_grad = sum_terms(pieces, left)[None]
    return (phase_rows, row_grad, weight_grad)


def solution(mesh):
    shape = dict(mesh.shape)
    side = math.isqrt(shape["seq"] // 2)
    fine = Mesh(
        mesh.devices.reshape(shape["phase"], side, side, 2, shape["dp"]),
        ("phase", "y", "x", "core", "dp"),
    )
    return jax.shard_map(
        body,
        mesh=fine,
        in_specs=(
            P("dp", SEQ, None),
            P(),
            P(),
            P(),
            P(),
            P(),
            P(),
            P(),
            P("phase", "dp", SEQ, None),
            P("phase", "dp", SEQ, None),
            P(),
            P("phase", "dp", SEQ, None, None),
            P("phase", "dp", SEQ, None, None),
            P("phase", "dp", SEQ, None),
        ),
        out_specs=(
            P("phase", "dp", SEQ, None),
            P("phase", "dp", SEQ, None),
            P("phase", None, SEQ + ("dp",), None),
        ),
        check_vma=False,
    )
```

```python
import functools
import math

import jax
import jax.numpy as jnp
from jax import lax
from jax.experimental import pallas as pl
from jax.experimental.pallas import tpu as pltpu
from jax.sharding import Mesh
from jax.sharding import PartitionSpec as P

DILATION_STEP = 2
SEQ = ("y", "x", "core")
F32 = jnp.float32
BF16 = jnp.bfloat16
I32 = jnp.int32
TAG = 128
NT = (((1,), (1,)), ((), ()))
TN = (((0,), (0,)), ((), ()))
VMEM = pl.BlockSpec(memory_space=pltpu.VMEM)
SMEM = pl.BlockSpec(memory_space=pltpu.SMEM)
ANY = pl.BlockSpec(memory_space=pl.ANY)
HBM = pl.BlockSpec(memory_space=pltpu.HBM)


def dot(a, b, dims=(((1,), (0,)), ((), ()))):
    return lax.dot_general(a, b, dims, preferred_element_type=F32)


def params(mib):
    return pltpu.CompilerParams(vmem_limit_bytes=mib << 20)


TOKEN = jax.ShapeDtypeStruct((8, 128), F32)


def cost(flops, nbytes):
    return pl.CostEstimate(flops=int(flops), bytes_accessed=int(nbytes), transcendentals=0)


def pick_kernel(
    ids_hbm,
    lines_hbm,
    counts_hbm,
    cot_hbm,
    out_ref,
    token_ref,
    ids_ref,
    lines_ref,
    counts_ref,
    cot_ref,
    sems,
):
    pairs = ((ids_hbm, ids_ref), (lines_hbm, lines_ref), (counts_hbm, counts_ref), (cot_hbm, cot_ref))
    copies = [
        pltpu.make_async_copy(source, target, sems.at[i])
        for i, (source, target) in enumerate(pairs)
    ]
    for copy in copies:
        copy.start()
    token_ref[...] = jnp.zeros_like(token_ref)
    batch, slots, shards = ids_ref.shape
    junc, embed = cot_ref.shape[1:]
    n = shards * slots
    owner = lax.broadcasted_iota(I32, (n, shards), 0) // slots
    spread = owner == lax.broadcasted_iota(I32, (n, shards), 1)
    spread16 = spread.astype(F32).astype(BF16)
    slot = lax.broadcasted_iota(I32, (n, slots), 0) % slots
    own = slot == lax.broadcasted_iota(I32, (n, slots), 1)

    def column(values):
        wide = dot(spread16, values.astype(F32).astype(BF16), NT)
        return jnp.sum(jnp.where(own, wide, 0.0), axis=1, keepdims=True)

    for copy in copies:
        copy.wait()
    tags = []
    for b in range(batch):
        ids = ids_ref[b]
        junction = column(ids % junc)
        code = column(ids // junc) * float(junc) + column(lines_ref[b])
        count = jnp.sum(
            jnp.where(spread, counts_ref[b : b + 1, :].astype(F32), 0.0), axis=1, keepdims=True
        )
        valid = slot[:, :1].astype(F32) < count
        junction = jnp.where(valid, junction, -1.0).astype(I32)
        tags.append(jnp.broadcast_to(jnp.where(valid, code, -1.0), (n, TAG)))
        onehot = (junction == lax.broadcasted_iota(I32, (n, junc), 1)).astype(F32).astype(BF16)
        picked = dot(onehot, cot_ref[b]).astype(BF16)
        out_ref[:, :, b * embed : (b + 1) * embed] = picked.reshape(shards, slots, embed)
    lane = lax.broadcasted_iota(I32, (n, TAG), 1)
    tag = tags[0]
    for b in range(1, batch):
        tag = jnp.where(lane < b * (TAG // batch), tag, tags[b])
    out_ref[:, :, batch * embed :] = tag.astype(BF16).reshape(shards, slots, TAG)


def pick(ids, lines, counts, cotangent):
    batch, slots, shards = ids.shape
    embed = cotangent.shape[2]
    return pl.pallas_call(
        pick_kernel,
        out_shape=(
            jax.ShapeDtypeStruct((shards, slots, batch * embed + TAG), BF16),
            TOKEN,
        ),
        in_specs=[ANY] * 4,
        out_specs=(VMEM, VMEM),
        scratch_shapes=[
            pltpu.VMEM(ids.shape, I32),
            pltpu.VMEM(lines.shape, I32),
            pltpu.VMEM(counts.shape, I32),
            pltpu.VMEM(cotangent.shape, BF16),
            pltpu.SemaphoreType.DMA((4,)),
        ],
        compiler_params=params(56),
        cost_estimate=cost(2 * 10**8, 3 * 10**6),
        name="pick",
    )(ids, lines, counts, cotangent)


def follow(value, *after):
    return pl.pallas_call(
        lambda *refs: None,
        out_shape=jax.ShapeDtypeStruct(value.shape, value.dtype),
        in_specs=[ANY] * (1 + len(after)),
        out_specs=ANY,
        input_output_aliases={0: 0},
        name="follow",
    )(value, *after)


def ends_kernel(arrived_ref, _token, _other, out_ref):
    shards, slots, wide = arrived_ref.shape
    embed = out_ref.shape[1] // 2
    batch = (wide - TAG) // embed
    n = shards * slots
    rows = out_ref.shape[0] // batch
    tags = arrived_ref[:, :, batch * embed :].reshape(n, TAG).astype(F32)
    for b in range(batch):
        data = arrived_ref[:, :, b * embed : (b + 1) * embed].reshape(n, embed)
        lane = b * (TAG // batch)
        tag = jnp.broadcast_to(tags[:, lane : lane + 1], (n, rows))
        for kind in range(2):
            target = lax.broadcasted_iota(I32, (n, rows), 1) + kind * rows
            onehot = (tag == target.astype(F32)).astype(F32).astype(BF16)
            out_ref[b * rows : (b + 1) * rows, kind * embed : (kind + 1) * embed] = dot(
                onehot, data, TN
            ).astype(BF16)


def make_ends(arrived, batch, rows, token, other):
    embed = (arrived.shape[2] - TAG) // batch
    return pl.pallas_call(
        ends_kernel,
        out_shape=jax.ShapeDtypeStruct((batch * rows, 2 * embed), BF16),
        in_specs=[VMEM, ANY, ANY],
        out_specs=VMEM,
        compiler_params=params(24),
        cost_estimate=cost(4 * 10**8, 3 * 10**6),
        name="ends",
    )(arrived, token, other)


def row_grad_kernel(ends_ref, head_ref, _token, out_ref):
    embed = head_ref.shape[2]
    total = dot(ends_ref[:, :embed], head_ref[0], NT)
    total = total + dot(ends_ref[:, embed:], head_ref[1], NT)
    out_ref[...] = total.astype(BF16)


def make_row_grad(ends, head, token):
    n, both = ends.shape
    width, embed = head.shape[1:]
    step = 512
    return pl.pallas_call(
        row_grad_kernel,
        grid=(width // step,),
        out_shape=jax.ShapeDtypeStruct((n, width), BF16),
        in_specs=[
            pl.BlockSpec((n, both), lambda i: (0, 0)),
            pl.BlockSpec((2, step, embed), lambda i: (0, i, 0)),
            ANY,
        ],
        out_specs=pl.BlockSpec((n, step), lambda i: (0, i)),
        compiler_params=params(24),
        cost_estimate=cost(1.2 * 10**9, 6 * 10**6),
        name="row_grad",
    )(ends, head, token)


def turn_kernel(place_ref, lines_ref, mine_ref, other_ref, turned):
    core, spot_y, spot_x = place_ref[0], place_ref[1], place_ref[2]
    blocks, part, n = mine_ref.shape
    side = math.isqrt(blocks)
    turned[...] = lines_ref[...].T.reshape(turned.shape)

    def block(core, k, i):
        on_x = i * side + lax.rem(spot_x + k, side)
        on_y = lax.rem(spot_y + k, side) * side + i
        return 2 * jnp.where(core == 0, on_x, on_y) + core

    for k in range(side):
        for i in range(side):
            mine_ref[k * side + i] = turned[block(core, k, i)]
            other_ref[k * side + i] = turned[block(1 - core, k, i)]


def turn(place, lines, blocks):
    n, width = lines.shape
    part = width // (2 * blocks)
    half = jax.ShapeDtypeStruct((blocks, part, n), BF16)
    return pl.pallas_call(
        turn_kernel,
        out_shape=(half, half),
        in_specs=[SMEM, VMEM],
        out_specs=(VMEM, VMEM),
        scratch_shapes=[pltpu.VMEM((2 * blocks, part, n), BF16)],
        compiler_params=params(24),
        cost_estimate=cost(10**6, 2 * 10**6),
        name="turn",
    )(place, lines)


def partial_kernel(mine_ref, other_ref, ends_ref, ends_other_ref, *out_refs):
    token_ref = out_refs[-1]
    token_ref[...] = jnp.zeros_like(token_ref)
    n = mine_ref.shape[2]
    count = len(out_refs) - 1
    step = mine_ref.shape[0] // count
    for i, out_ref in enumerate(out_refs[:-1]):
        rows = out_ref.shape[0]
        span = slice(i * step, (i + 1) * step)
        total = dot(mine_ref[span].reshape(rows, n), ends_ref[...])
        total = total + dot(other_ref[span].reshape(rows, n), ends_other_ref[...])
        out_ref[...] = total.astype(BF16)


def partial_grad(mine, other, ends, ends_other, side):
    rows, width = mine.shape[0] * mine.shape[1], ends.shape[1]
    piece = jax.ShapeDtypeStruct((rows // side, width), BF16)
    return pl.pallas_call(
        partial_kernel,
        out_shape=(piece,) * side + (TOKEN,),
        in_specs=[VMEM] * 4,
        out_specs=(VMEM,) * (side + 1),
        compiler_params=params(24),
        cost_estimate=cost(1.2 * 10**9, 5 * 10**6),
        name="partial_grad",
    )(mine, other, ends, ends_other)


def line_sum_kernel(*refs):
    pieces, out_ref = refs[:-2], refs[-1]
    total = functools.reduce(jnp.add, [piece[...].astype(F32) for piece in pieces])
    out_ref[...] = total.astype(BF16).reshape(out_ref.shape)


def line_sum(pieces, count, after):
    rows, width = pieces[0].shape
    return pl.pallas_call(
        line_sum_kernel,
        out_shape=jax.ShapeDtypeStruct((count, rows // count, width), BF16),
        in_specs=[VMEM] * len(pieces) + [ANY],
        out_specs=VMEM,
        compiler_params=params(24),
        cost_estimate=cost(10**6, 3 * 10**6),
        name="line_sum",
    )(*pieces, after)


def encoder_kernel(
    core_ref,
    low_ref,
    high_ref,
    gain_ref,
    x_hbm,
    taps_hbm,
    merge_hbm,
    look_hbm,
    ask_hbm,
    after_ref,
    rows_hbm,
    key_own_ref,
    key_out_ref,
    query_own_ref,
    query_out_ref,
    token_ref,
    x_ref,
    taps,
    merge,
    look,
    ask,
    pad,
    hidden,
    rows_ref,
    sems,
):
    pairs = ((x_hbm, x_ref), (taps_hbm, taps), (merge_hbm, merge), (look_hbm, look), (ask_hbm, ask))
    copies = [
        pltpu.make_async_copy(source, target, sems.at[i])
        for i, (source, target) in enumerate(pairs)
    ]
    for copy in copies:
        copy.start()
    out_copy = pltpu.make_async_copy(rows_ref, rows_hbm, sems.at[len(pairs)])
    batch, cells, chans = x_ref.shape
    extent = low_ref.shape[1]
    base = 8
    copies[0].wait()
    for b in range(batch):
        pad[b, base - extent : base, :] = low_ref[b].astype(F32)
        pad[b, base : base + cells, :] = x_ref[b].astype(F32)
        pad[b, base + cells : base + cells + extent, :] = high_ref[b].astype(F32)
    copies[1].wait()
    for b in range(batch):
        before = pad[b, base - extent : base - extent + cells, :].astype(BF16)
        behind = pad[b, base + extent : base + extent + cells, :].astype(BF16)
        for j in range(0, chans, 256):
            span = slice(j, j + 256)
            total = dot(x_ref[b], taps[1, :, span])
            total += dot(before, taps[0, :, span]) + dot(behind, taps[2, :, span])
            total = pad[b, base : base + cells, span] + jax.nn.gelu(total)
            for i in range(0, 256, 128):
                hidden[(j + i) // 128, b * cells : (b + 1) * cells, :] = total[:, i : i + 128]
    n = batch * cells // 2
    pooled = jnp.concatenate(
        [
            ((hidden[j, pl.ds(0, n, 2), :] + hidden[j, pl.ds(1, n, 2), :]) * 0.5).astype(BF16)
            for j in range(hidden.shape[0])
        ],
        axis=1,
    )
    copies[2].wait()
    rows = dot(pooled, merge[...]).astype(BF16)
    rows_ref[...] = rows
    out_copy.start()
    wide = rows.astype(F32)
    scale = lax.rsqrt(jnp.mean(wide * wide, axis=-1, keepdims=True) + 1e-06)
    normed = (wide * scale * gain_ref[...]).astype(BF16)
    half = n // 2
    first = core_ref[0] == 0

    def halves(value, own_ref, out_ref):
        own_ref[...] = jnp.where(first, value[:half], value[half:])
        out_ref[...] = jnp.where(first, value[half:], value[:half])

    copies[3].wait()
    halves(dot(normed, look[...]).astype(BF16), key_own_ref, key_out_ref)
    copies[4].wait()
    halves(dot(normed, ask[...]).astype(BF16), query_own_ref, query_out_ref)
    token_ref[...] = jnp.zeros_like(token_ref)
    out_copy.wait()


def encode(core, x, low, high, gain, taps, merge, look, ask, after):
    batch, cells, chans = x.shape
    n = batch * cells // 2
    width = merge.shape[1]
    key = jax.ShapeDtypeStruct((n // 2, look.shape[1]), BF16)
    query = jax.ShapeDtypeStruct((n // 2, ask.shape[1]), BF16)
    return pl.pallas_call(
        encoder_kernel,
        out_shape=(jax.ShapeDtypeStruct((n, width), BF16), key, key, query, query, TOKEN),
        in_specs=[SMEM] + [VMEM] * 3 + [HBM] * 5 + [ANY],
        out_specs=(HBM,) + (VMEM,) * 5,
        scratch_shapes=[
            pltpu.VMEM(x.shape, BF16),
            pltpu.VMEM(taps.shape, BF16),
            pltpu.VMEM(merge.shape, BF16),
            pltpu.VMEM(look.shape, BF16),
            pltpu.VMEM(ask.shape, BF16),
            pltpu.VMEM((batch, cells + 16, chans), F32),
            pltpu.VMEM((chans // 128, batch * cells, 128), F32),
            pltpu.VMEM((n, width), BF16),
            pltpu.SemaphoreType.DMA((6,)),
        ],
        compiler_params=params(56),
        cost_estimate=cost(3.4 * 10**9, 12 * 10**6),
        name="encode",
    )(core.reshape(1), low, high, gain.reshape(1, width), x, taps, merge, look, ask, after)


def attend_part(logit_ref, query_own_ref, query_in_ref, keys, key_t, value, put):
    rows, width = query_own_ref.shape
    n, both = keys[0].shape
    lane = both // 2
    count = n * len(keys)
    chunk = 512
    for i, block in enumerate(keys):
        span = slice(i * n, (i + 1) * n)
        turned = block[:, :lane].T
        key_t[:lane, span] = turned
        key_t[lane:, span] = turned
        value[span, :lane] = block[:, lane:]
        value[span, lane:] = jnp.ones((n, lane), BF16)
    for head in range(width // lane):
        span = slice(head * lane, (head + 1) * lane)
        query = jnp.concatenate([query_own_ref[:, span], query_in_ref[:, span]], axis=0)
        query = query.astype(F32) * logit_ref[head]
        coarse = query.astype(BF16)
        fine = (query - coarse.astype(F32)).astype(BF16)
        query = jnp.concatenate([coarse, fine], axis=1)
        scores = [dot(query, key_t[:, j : j + chunk]) for j in range(0, count, chunk)]
        top = jnp.max(functools.reduce(jnp.maximum, scores), axis=-1, keepdims=True)
        mixed = 0.0
        for j, score in enumerate(scores):
            weight = jnp.exp2(score - top).astype(BF16)
            mixed = mixed + dot(weight, value[j * chunk : (j + 1) * chunk, :])
        put(span, mixed[:, :lane], mixed[:, lane:], jnp.broadcast_to(top, (2 * rows, lane)))


def attend_first_kernel(phase_ref, logit_ref, query_own_ref, query_in_ref, *refs):
    keys, (_, mixed_ref, total_ref, top_ref, key_t, value) = refs[:-6], refs[-6:]

    @pl.when(phase_ref[0] == 1)
    def _():
        def put(span, mixed, total, top):
            mixed_ref[:, span] = mixed
            total_ref[:, span] = total
            top_ref[:, span] = top

        attend_part(logit_ref, query_own_ref, query_in_ref, keys, key_t, value, put)


def attend_first(phase, logit, query_own, query_in, keys, after):
    n, both = keys[0].shape
    count = n * len(keys)
    rows, width = query_own.shape
    part = jax.ShapeDtypeStruct((2 * rows, width), F32)
    return pl.pallas_call(
        attend_first_kernel,
        out_shape=(part, part, part),
        in_specs=[SMEM, SMEM] + [VMEM] * (2 + len(keys)) + [ANY],
        out_specs=(VMEM,) * 3,
        scratch_shapes=[pltpu.VMEM((both, count), BF16), pltpu.VMEM((count, both), BF16)],
        compiler_params=params(28),
        cost_estimate=cost(10**9, 4 * 10**6),
        name="attend_first",
    )(phase.reshape(1), logit, query_own, query_in, *keys, after)


def attend_rest_kernel(
    phase_ref, logit_ref, query_own_ref, query_in_ref, mixed_ref, total_ref, top_ref, *refs
):
    keys, (own_ref, out_ref, token_ref, key_t, value) = refs[:-5], refs[-5:]
    token_ref[...] = jnp.zeros_like(token_ref)
    rows = query_own_ref.shape[0]

    @pl.when(phase_ref[0] == 1)
    def _():
        def put(span, mixed, total, top):
            highest = jnp.maximum(top, top_ref[:, span])
            here, there = jnp.exp2(top - highest), jnp.exp2(top_ref[:, span] - highest)
            mixed = mixed * here + mixed_ref[:, span] * there
            total = total * here + total_ref[:, span] * there
            mixed = (mixed / total).astype(BF16)
            own_ref[:, span] = mixed[:rows]
            out_ref[:, span] = mixed[rows:]

        attend_part(logit_ref, query_own_ref, query_in_ref, keys, key_t, value, put)


def attend_rest(phase, logit, query_own, query_in, parts, keys):
    shape = jax.ShapeDtypeStruct(query_own.shape, BF16)
    n, both = keys[0].shape
    count = n * len(keys)
    return pl.pallas_call(
        attend_rest_kernel,
        out_shape=(shape, shape, TOKEN),
        in_specs=[SMEM, SMEM] + [VMEM] * (5 + len(keys)),
        out_specs=(VMEM, VMEM, VMEM),
        scratch_shapes=[pltpu.VMEM((both, count), BF16), pltpu.VMEM((count, both), BF16)],
        compiler_params=params(28),
        cost_estimate=cost(6 * 10**10, 4 * 10**6),
        name="attend_rest",
    )(phase.reshape(1), logit, query_own, query_in, *parts, *keys)


def exit_kernel(phase_ref, core_ref, rows_ref, own_ref, in_ref, exit_ref, out_ref, token_ref):
    token_ref[...] = jnp.zeros_like(token_ref)
    n = own_ref.shape[0]
    on = phase_ref[0] == 1

    @pl.when(on)
    def _():
        attended = jnp.concatenate([own_ref[...], in_ref[...]], axis=0)
        mixed = dot(attended, exit_ref[...])
        for i in range(2):
            owner = core_ref[0] if i == 0 else 1 - core_ref[0]
            span = pl.ds(pl.multiple_of(owner * n, n), n)
            out_ref[span, :] = (rows_ref[span, :].astype(F32) + mixed[i * n : (i + 1) * n]).astype(
                BF16
            )

    @pl.when(jnp.logical_not(on))
    def _():
        out_ref[...] = rows_ref[...]


def leave(phase, core, encoded, own, arrived, exit_projector):
    return pl.pallas_call(
        exit_kernel,
        out_shape=(jax.ShapeDtypeStruct(encoded.shape, BF16), TOKEN),
        in_specs=[SMEM, SMEM] + [VMEM] * 4,
        out_specs=(VMEM, VMEM),
        compiler_params=params(32),
        cost_estimate=cost(8 * 10**8, 5 * 10**6),
        name="leave",
    )(phase.reshape(1), core.reshape(1), encoded, own, arrived, exit_projector)


def gather_terms_kernel(pieces_ref, _, out_ref):
    embed = out_ref.shape[2]
    total = jnp.sum(pieces_ref[...].astype(F32), axis=0)
    for kind in range(2):
        out_ref[kind] = total[:, kind * embed : (kind + 1) * embed]


def sum_terms(pieces, after):
    _, rows, width = pieces.shape
    return pl.pallas_call(
        gather_terms_kernel,
        out_shape=jax.ShapeDtypeStruct((2, rows, width // 2), F32),
        in_specs=[VMEM, ANY],
        out_specs=VMEM,
        compiler_params=params(32),
        cost_estimate=cost(10**6, 3 * 10**6),
        name="sum_terms",
    )(pieces, after)


def stack_kernel(*refs):
    blocks, (out_ref, token_ref) = refs[:-2], refs[-2:]
    rows = blocks[0].shape[0]
    for i, block in enumerate(blocks):
        out_ref[i * rows : (i + 1) * rows, :] = block[...]
    token_ref[...] = jnp.zeros_like(token_ref)


def stack(blocks):
    rows, width = blocks[0].shape
    return pl.pallas_call(
        stack_kernel,
        out_shape=(jax.ShapeDtypeStruct((len(blocks) * rows, width), BF16), TOKEN),
        in_specs=[VMEM] * len(blocks),
        out_specs=(VMEM, VMEM),
        compiler_params=params(8),
        cost_estimate=cost(10**5, 10**6),
        name="stack",
    )(*blocks)


def line_pairs(side, first, distance):
    pairs = []
    for y in range(side):
        for x in range(side):
            for core in range(2):
                along_x = (core == 0) == first
                to_x = (x + distance) % side if along_x else x
                to_y = y if along_x else (y + distance) % side
                pairs.append(((y * side + x) * 2 + core, (to_y * side + to_x) * 2 + core))
    return pairs


def lines_of(side, first, depth):
    groups = []
    for i in range(side):
        for core in range(2):
            along_x = (core == 0) == first
            chips = [i * side + k if along_x else k * side + i for k in range(side)]
            groups.append([(chip * 2 + core) * depth + d for chip in chips for d in range(depth)])
    return groups


def spread(block, side, first):
    return [
        lax.ppermute(block, SEQ, line_pairs(side, first, distance))
        for distance in (1, side - 1, 2)
    ]


def halo(first, last):
    count = lax.axis_size(SEQ)
    forward = [(i, i + 1) for i in range(count - 1)]
    backward = [(b, a) for a, b in forward]
    return lax.ppermute(last, SEQ, forward), lax.ppermute(first, SEQ, backward)


def body(
    bin_activations,
    spaced_filter_coefs,
    merged_bin_projector,
    backbone_rms_gain,
    asking_projector,
    common_lookup_projector,
    attention_exit_projector,
    lane_logit_factor,
    splice_readout_lines,
    couple_embedding_cotangent,
    splice_site_projector,
    site_locator_code,
    site_local_line,
    filled_slot_totals,
):
    phase = lax.axis_index("phase")
    core = lax.axis_index("core")
    batch, cells, chans = bin_activations.shape
    rows = cells // 2
    width = merged_bin_projector.shape[1]
    extent = DILATION_STEP * (spaced_filter_coefs.shape[0] // 2)
    lane = common_lookup_projector.shape[1] // 2
    shards = site_locator_code.shape[3]
    swap = [(0, 1), (1, 0)]
    side = lax.axis_size("y")

    first, last = bin_activations[:, :extent], bin_activations[:, -extent:]
    low, high = halo(first, last)
    payload, picked = pick(
        jnp.swapaxes(site_locator_code[0, :, 0], 1, 2),
        jnp.swapaxes(site_local_line[0, :, 0], 1, 2),
        filled_slot_totals[0, :, 0],
        couple_embedding_cotangent[0],
    )
    payload = follow(payload, low, high)
    arrived = lax.all_to_all(payload, SEQ, 0, 0, tiled=True)

    encoded, key_own, key_out, query_own, query_out, _ = encode(
        core,
        bin_activations,
        low,
        high,
        backbone_rms_gain,
        spaced_filter_coefs,
        merged_bin_projector,
        common_lookup_projector,
        asking_projector,
        picked,
    )
    chip_keys, _ = stack([key_own, lax.ppermute(key_out, "core", swap)])
    line_keys, line_done = stack([chip_keys] + spread(chip_keys, side, True))
    keys = [line_keys] + spread(line_keys, side, False)
    query_in = lax.ppermute(query_out, "core", swap)

    portion = splice_readout_lines[0].reshape(batch * rows, width)
    place = jnp.stack([core, lax.axis_index("y"), lax.axis_index("x")]).astype(I32)
    mine, other = turn(place, portion, shards // 2)
    other = lax.ppermute(other, "core", swap)

    ends = make_ends(arrived, batch, rows, line_done, other)
    ends_other = lax.ppermute(ends, "core", swap)
    *partial, terms_done = partial_grad(mine, other, ends, ends_other, side)
    terms = [partial[0]] + [
        lax.ppermute(partial[k], SEQ, line_pairs(side, True, k)) for k in (1, side - 1, 2)
    ]

    row_grad = make_row_grad(ends, splice_site_projector, terms_done)
    row_grad = row_grad.reshape(batch, rows, width)[None]

    logit = lane_logit_factor * (math.log2(math.e) / math.sqrt(lane))
    parts = attend_first(phase, logit, query_own, query_in, keys[:2], terms_done)
    own, out, attended = attend_rest(phase, logit, query_own, query_in, parts, keys[2:])
    rows_out, left = leave(
        phase, core, encoded, own, lax.ppermute(out, "core", swap), attention_exit_projector
    )
    phase_rows = rows_out.reshape(batch, rows, width)[None]

    depth = lax.axis_size("dp")
    line_terms = line_sum(terms, side * depth, attended)
    pieces = lax.all_to_all(
        line_terms,
        SEQ + ("dp",),
        0,
        0,
        axis_index_groups=lines_of(side, False, depth),
        tiled=True,
    )
    weight_grad = sum_terms(pieces, left)[None]
    return (phase_rows, row_grad, weight_grad)


def solution(mesh):
    shape = dict(mesh.shape)
    side = math.isqrt(shape["seq"] // 2)
    fine = Mesh(
        mesh.devices.reshape(shape["phase"], side, side, 2, shape["dp"]),
        ("phase", "y", "x", "core", "dp"),
    )
    return jax.shard_map(
        body,
        mesh=fine,
        in_specs=(
            P("dp", SEQ, None),
            P(),
            P(),
            P(),
            P(),
            P(),
            P(),
            P(),
            P("phase", "dp", SEQ, None),
            P("phase", "dp", SEQ, None),
            P(),
            P("phase", "dp", SEQ, None, None),
            P("phase", "dp", SEQ, None, None),
            P("phase", "dp", SEQ, None),
        ),
        out_specs=(
            P("phase", "dp", SEQ, None),
            P("phase", "dp", SEQ, None),
            P("phase", None, SEQ + ("dp",), None),
        ),
        check_vma=False,
    )
```

```python
import functools
import math

import jax
import jax.numpy as jnp
from jax import lax
from jax.experimental import pallas as pl
from jax.experimental.pallas import tpu as pltpu
from jax.sharding import Mesh
from jax.sharding import PartitionSpec as P

DILATION_STEP = 2
SEQ = ("y", "x", "core")
F32 = jnp.float32
BF16 = jnp.bfloat16
I32 = jnp.int32
TAG = 128
NT = (((1,), (1,)), ((), ()))
TN = (((0,), (0,)), ((), ()))
VMEM = pl.BlockSpec(memory_space=pltpu.VMEM)
SMEM = pl.BlockSpec(memory_space=pltpu.SMEM)
ANY = pl.BlockSpec(memory_space=pl.ANY)
HBM = pl.BlockSpec(memory_space=pltpu.HBM)


def dot(a, b, dims=(((1,), (0,)), ((), ()))):
    return lax.dot_general(a, b, dims, preferred_element_type=F32)


def params(mib):
    return pltpu.CompilerParams(vmem_limit_bytes=mib << 20)


TOKEN = jax.ShapeDtypeStruct((8, 128), F32)


def cost(flops, nbytes):
    return pl.CostEstimate(flops=int(flops), bytes_accessed=int(nbytes), transcendentals=0)


def pick_kernel(
    ids_hbm,
    lines_hbm,
    counts_hbm,
    cot_hbm,
    out_ref,
    token_ref,
    ids_ref,
    lines_ref,
    counts_ref,
    cot_ref,
    sems,
):
    pairs = ((ids_hbm, ids_ref), (lines_hbm, lines_ref), (counts_hbm, counts_ref), (cot_hbm, cot_ref))
    copies = [
        pltpu.make_async_copy(source, target, sems.at[i])
        for i, (source, target) in enumerate(pairs)
    ]
    for copy in copies:
        copy.start()
    token_ref[...] = jnp.zeros_like(token_ref)
    batch, slots, shards = ids_ref.shape
    junc, embed = cot_ref.shape[1:]
    n = shards * slots
    owner = lax.broadcasted_iota(I32, (n, shards), 0) // slots
    spread = owner == lax.broadcasted_iota(I32, (n, shards), 1)
    spread16 = spread.astype(F32).astype(BF16)
    slot = lax.broadcasted_iota(I32, (n, slots), 0) % slots
    own = slot == lax.broadcasted_iota(I32, (n, slots), 1)

    def column(values):
        wide = dot(spread16, values.astype(F32).astype(BF16), NT)
        return jnp.sum(jnp.where(own, wide, 0.0), axis=1, keepdims=True)

    for copy in copies:
        copy.wait()
    tags = []
    for b in range(batch):
        ids = ids_ref[b]
        junction = column(ids % junc)
        code = column(ids // junc) * float(junc) + column(lines_ref[b])
        count = jnp.sum(
            jnp.where(spread, counts_ref[b : b + 1, :].astype(F32), 0.0), axis=1, keepdims=True
        )
        valid = slot[:, :1].astype(F32) < count
        junction = jnp.where(valid, junction, -1.0).astype(I32)
        tags.append(jnp.broadcast_to(jnp.where(valid, code, -1.0), (n, TAG)))
        onehot = (junction == lax.broadcasted_iota(I32, (n, junc), 1)).astype(F32).astype(BF16)
        picked = dot(onehot, cot_ref[b]).astype(BF16)
        out_ref[:, :, b * embed : (b + 1) * embed] = picked.reshape(shards, slots, embed)
    lane = lax.broadcasted_iota(I32, (n, TAG), 1)
    tag = tags[0]
    for b in range(1, batch):
        tag = jnp.where(lane < b * (TAG // batch), tag, tags[b])
    out_ref[:, :, batch * embed :] = tag.astype(BF16).reshape(shards, slots, TAG)


def pick(ids, lines, counts, cotangent):
    batch, slots, shards = ids.shape
    embed = cotangent.shape[2]
    return pl.pallas_call(
        pick_kernel,
        out_shape=(
            jax.ShapeDtypeStruct((shards, slots, batch * embed + TAG), BF16),
            TOKEN,
        ),
        in_specs=[ANY] * 4,
        out_specs=(VMEM, VMEM),
        scratch_shapes=[
            pltpu.VMEM(ids.shape, I32),
            pltpu.VMEM(lines.shape, I32),
            pltpu.VMEM(counts.shape, I32),
            pltpu.VMEM(cotangent.shape, BF16),
            pltpu.SemaphoreType.DMA((4,)),
        ],
        compiler_params=params(56),
        cost_estimate=cost(2 * 10**8, 3 * 10**6),
        name="pick",
    )(ids, lines, counts, cotangent)


def follow(value, *after):
    return pl.pallas_call(
        lambda *refs: None,
        out_shape=jax.ShapeDtypeStruct(value.shape, value.dtype),
        in_specs=[ANY] * (1 + len(after)),
        out_specs=ANY,
        input_output_aliases={0: 0},
        name="follow",
    )(value, *after)


def ends_kernel(arrived_ref, _token, _other, out_ref):
    shards, slots, wide = arrived_ref.shape
    embed = out_ref.shape[1] // 2
    batch = (wide - TAG) // embed
    n = shards * slots
    rows = out_ref.shape[0] // batch
    tags = arrived_ref[:, :, batch * embed :].reshape(n, TAG).astype(F32)
    for b in range(batch):
        data = arrived_ref[:, :, b * embed : (b + 1) * embed].reshape(n, embed)
        lane = b * (TAG // batch)
        tag = jnp.broadcast_to(tags[:, lane : lane + 1], (n, rows))
        for kind in range(2):
            target = lax.broadcasted_iota(I32, (n, rows), 1) + kind * rows
            onehot = (tag == target.astype(F32)).astype(F32).astype(BF16)
            out_ref[b * rows : (b + 1) * rows, kind * embed : (kind + 1) * embed] = dot(
                onehot, data, TN
            ).astype(BF16)


def make_ends(arrived, batch, rows, token, other):
    embed = (arrived.shape[2] - TAG) // batch
    return pl.pallas_call(
        ends_kernel,
        out_shape=jax.ShapeDtypeStruct((batch * rows, 2 * embed), BF16),
        in_specs=[VMEM, ANY, ANY],
        out_specs=VMEM,
        compiler_params=params(24),
        cost_estimate=cost(4 * 10**8, 3 * 10**6),
        name="ends",
    )(arrived, token, other)


def row_grad_kernel(ends_ref, head_ref, _token, out_ref):
    embed = head_ref.shape[2]
    total = dot(ends_ref[:, :embed], head_ref[0], NT)
    total = total + dot(ends_ref[:, embed:], head_ref[1], NT)
    out_ref[...] = total.astype(BF16)


def make_row_grad(ends, head, token):
    n, both = ends.shape
    width, embed = head.shape[1:]
    step = 512
    return pl.pallas_call(
        row_grad_kernel,
        grid=(width // step,),
        out_shape=jax.ShapeDtypeStruct((n, width), BF16),
        in_specs=[
            pl.BlockSpec((n, both), lambda i: (0, 0)),
            pl.BlockSpec((2, step, embed), lambda i: (0, i, 0)),
            ANY,
        ],
        out_specs=pl.BlockSpec((n, step), lambda i: (0, i)),
        compiler_params=params(24),
        cost_estimate=cost(1.2 * 10**9, 6 * 10**6),
        name="row_grad",
    )(ends, head, token)


def turn_kernel(place_ref, lines_ref, _token, mine_ref, other_ref, turned):
    core, spot_y, spot_x = place_ref[0], place_ref[1], place_ref[2]
    blocks, part, n = mine_ref.shape
    side = math.isqrt(blocks)
    turned[...] = lines_ref[...].T.reshape(turned.shape)

    def block(core, k, i):
        on_x = i * side + lax.rem(spot_x + k, side)
        on_y = lax.rem(spot_y + k, side) * side + i
        return 2 * jnp.where(core == 0, on_x, on_y) + core

    for k in range(side):
        for i in range(side):
            mine_ref[k * side + i] = turned[block(core, k, i)]
            other_ref[k * side + i] = turned[block(1 - core, k, i)]


def turn(place, lines, blocks, after):
    n, width = lines.shape
    part = width // (2 * blocks)
    half = jax.ShapeDtypeStruct((blocks, part, n), BF16)
    return pl.pallas_call(
        turn_kernel,
        out_shape=(half, half),
        in_specs=[SMEM, VMEM, ANY],
        out_specs=(VMEM, VMEM),
        scratch_shapes=[pltpu.VMEM((2 * blocks, part, n), BF16)],
        compiler_params=params(24),
        cost_estimate=cost(10**6, 2 * 10**6),
        name="turn",
    )(place, lines, after)


def partial_kernel(mine_ref, other_ref, ends_ref, ends_other_ref, *out_refs):
    token_ref = out_refs[-1]
    token_ref[...] = jnp.zeros_like(token_ref)
    n = mine_ref.shape[2]
    count = len(out_refs) - 1
    step = mine_ref.shape[0] // count
    for i, out_ref in enumerate(out_refs[:-1]):
        rows = out_ref.shape[0]
        span = slice(i * step, (i + 1) * step)
        total = dot(mine_ref[span].reshape(rows, n), ends_ref[...])
        total = total + dot(other_ref[span].reshape(rows, n), ends_other_ref[...])
        out_ref[...] = total.astype(BF16)


def partial_grad(mine, other, ends, ends_other, side):
    rows, width = mine.shape[0] * mine.shape[1], ends.shape[1]
    piece = jax.ShapeDtypeStruct((rows // side, width), BF16)
    return pl.pallas_call(
        partial_kernel,
        out_shape=(piece,) * side + (TOKEN,),
        in_specs=[VMEM] * 4,
        out_specs=(VMEM,) * (side + 1),
        compiler_params=params(24),
        cost_estimate=cost(1.2 * 10**9, 5 * 10**6),
        name="partial_grad",
    )(mine, other, ends, ends_other)


def line_sum_kernel(*refs):
    pieces, out_ref = refs[:-2], refs[-1]
    total = functools.reduce(jnp.add, [piece[...].astype(F32) for piece in pieces])
    out_ref[...] = total.astype(BF16).reshape(out_ref.shape)


def line_sum(pieces, count, after):
    rows, width = pieces[0].shape
    return pl.pallas_call(
        line_sum_kernel,
        out_shape=jax.ShapeDtypeStruct((count, rows // count, width), BF16),
        in_specs=[VMEM] * len(pieces) + [ANY],
        out_specs=VMEM,
        compiler_params=params(24),
        cost_estimate=cost(10**6, 3 * 10**6),
        name="line_sum",
    )(*pieces, after)


def encoder_kernel(
    core_ref,
    low_ref,
    high_ref,
    gain_ref,
    x_hbm,
    taps_hbm,
    merge_hbm,
    look_hbm,
    ask_hbm,
    after_ref,
    rows_hbm,
    key_own_ref,
    key_out_ref,
    query_own_ref,
    query_out_ref,
    token_ref,
    x_ref,
    taps,
    merge,
    look,
    ask,
    pad,
    hidden,
    rows_ref,
    sems,
):
    pairs = ((x_hbm, x_ref), (taps_hbm, taps), (merge_hbm, merge), (look_hbm, look), (ask_hbm, ask))
    copies = [
        pltpu.make_async_copy(source, target, sems.at[i])
        for i, (source, target) in enumerate(pairs)
    ]
    for copy in copies:
        copy.start()
    out_copy = pltpu.make_async_copy(rows_ref, rows_hbm, sems.at[len(pairs)])
    batch, cells, chans = x_ref.shape
    extent = low_ref.shape[1]
    base = 8
    copies[0].wait()
    for b in range(batch):
        pad[b, base - extent : base, :] = low_ref[b].astype(F32)
        pad[b, base : base + cells, :] = x_ref[b].astype(F32)
        pad[b, base + cells : base + cells + extent, :] = high_ref[b].astype(F32)
    copies[1].wait()
    for b in range(batch):
        before = pad[b, base - extent : base - extent + cells, :].astype(BF16)
        behind = pad[b, base + extent : base + extent + cells, :].astype(BF16)
        for j in range(0, chans, 256):
            span = slice(j, j + 256)
            total = dot(x_ref[b], taps[1, :, span])
            total += dot(before, taps[0, :, span]) + dot(behind, taps[2, :, span])
            total = pad[b, base : base + cells, span] + jax.nn.gelu(total)
            for i in range(0, 256, 128):
                hidden[(j + i) // 128, b * cells : (b + 1) * cells, :] = total[:, i : i + 128]
    n = batch * cells // 2
    pooled = jnp.concatenate(
        [
            ((hidden[j, pl.ds(0, n, 2), :] + hidden[j, pl.ds(1, n, 2), :]) * 0.5).astype(BF16)
            for j in range(hidden.shape[0])
        ],
        axis=1,
    )
    copies[2].wait()
    rows = dot(pooled, merge[...]).astype(BF16)
    rows_ref[...] = rows
    out_copy.start()
    wide = rows.astype(F32)
    scale = lax.rsqrt(jnp.mean(wide * wide, axis=-1, keepdims=True) + 1e-06)
    normed = (wide * scale * gain_ref[...]).astype(BF16)
    half = n // 2
    first = core_ref[0] == 0

    def halves(value, own_ref, out_ref):
        own_ref[...] = jnp.where(first, value[:half], value[half:])
        out_ref[...] = jnp.where(first, value[half:], value[:half])

    copies[3].wait()
    halves(dot(normed, look[...]).astype(BF16), key_own_ref, key_out_ref)
    copies[4].wait()
    halves(dot(normed, ask[...]).astype(BF16), query_own_ref, query_out_ref)
    token_ref[...] = jnp.zeros_like(token_ref)
    out_copy.wait()


def encode(core, x, low, high, gain, taps, merge, look, ask, after):
    batch, cells, chans = x.shape
    n = batch * cells // 2
    width = merge.shape[1]
    key = jax.ShapeDtypeStruct((n // 2, look.shape[1]), BF16)
    query = jax.ShapeDtypeStruct((n // 2, ask.shape[1]), BF16)
    return pl.pallas_call(
        encoder_kernel,
        out_shape=(jax.ShapeDtypeStruct((n, width), BF16), key, key, query, query, TOKEN),
        in_specs=[SMEM] + [VMEM] * 3 + [HBM] * 5 + [ANY],
        out_specs=(HBM,) + (VMEM,) * 5,
        scratch_shapes=[
            pltpu.VMEM(x.shape, BF16),
            pltpu.VMEM(taps.shape, BF16),
            pltpu.VMEM(merge.shape, BF16),
            pltpu.VMEM(look.shape, BF16),
            pltpu.VMEM(ask.shape, BF16),
            pltpu.VMEM((batch, cells + 16, chans), F32),
            pltpu.VMEM((chans // 128, batch * cells, 128), F32),
            pltpu.VMEM((n, width), BF16),
            pltpu.SemaphoreType.DMA((6,)),
        ],
        compiler_params=params(56),
        cost_estimate=cost(3.4 * 10**9, 12 * 10**6),
        name="encode",
    )(core.reshape(1), low, high, gain.reshape(1, width), x, taps, merge, look, ask, after)


def attend_part(logit_ref, query_own_ref, query_in_ref, keys, key_t, value, put):
    rows, width = query_own_ref.shape
    n, both = keys[0].shape
    lane = both // 2
    count = n * len(keys)
    chunk = 512
    for i, block in enumerate(keys):
        span = slice(i * n, (i + 1) * n)
        turned = block[:, :lane].T
        key_t[:lane, span] = turned
        key_t[lane:, span] = turned
        value[span, :lane] = block[:, lane:]
        value[span, lane:] = jnp.ones((n, lane), BF16)
    for head in range(width // lane):
        span = slice(head * lane, (head + 1) * lane)
        query = jnp.concatenate([query_own_ref[:, span], query_in_ref[:, span]], axis=0)
        query = query.astype(F32) * logit_ref[head]
        coarse = query.astype(BF16)
        fine = (query - coarse.astype(F32)).astype(BF16)
        query = jnp.concatenate([coarse, fine], axis=1)
        scores = [dot(query, key_t[:, j : j + chunk]) for j in range(0, count, chunk)]
        top = jnp.max(functools.reduce(jnp.maximum, scores), axis=-1, keepdims=True)
        mixed = 0.0
        for j, score in enumerate(scores):
            weight = jnp.exp2(score - top).astype(BF16)
            mixed = mixed + dot(weight, value[j * chunk : (j + 1) * chunk, :])
        put(span, mixed[:, :lane], mixed[:, lane:], jnp.broadcast_to(top, (2 * rows, lane)))


def attend_first_kernel(phase_ref, logit_ref, query_own_ref, query_in_ref, *refs):
    keys, (_, mixed_ref, total_ref, top_ref, key_t, value) = refs[:-6], refs[-6:]

    @pl.when(phase_ref[0] == 1)
    def _():
        def put(span, mixed, total, top):
            mixed_ref[:, span] = mixed
            total_ref[:, span] = total
            top_ref[:, span] = top

        attend_part(logit_ref, query_own_ref, query_in_ref, keys, key_t, value, put)


def attend_first(phase, logit, query_own, query_in, keys, after):
    n, both = keys[0].shape
    count = n * len(keys)
    rows, width = query_own.shape
    part = jax.ShapeDtypeStruct((2 * rows, width), F32)
    return pl.pallas_call(
        attend_first_kernel,
        out_shape=(part, part, part),
        in_specs=[SMEM, SMEM] + [VMEM] * (2 + len(keys)) + [ANY],
        out_specs=(VMEM,) * 3,
        scratch_shapes=[pltpu.VMEM((both, count), BF16), pltpu.VMEM((count, both), BF16)],
        compiler_params=params(28),
        cost_estimate=cost(10**9, 4 * 10**6),
        name="attend_first",
    )(phase.reshape(1), logit, query_own, query_in, *keys, after)


def attend_rest_kernel(
    phase_ref, logit_ref, query_own_ref, query_in_ref, mixed_ref, total_ref, top_ref, *refs
):
    keys, (own_ref, out_ref, token_ref, key_t, value) = refs[:-5], refs[-5:]
    token_ref[...] = jnp.zeros_like(token_ref)
    rows = query_own_ref.shape[0]

    @pl.when(phase_ref[0] == 1)
    def _():
        def put(span, mixed, total, top):
            highest = jnp.maximum(top, top_ref[:, span])
            here, there = jnp.exp2(top - highest), jnp.exp2(top_ref[:, span] - highest)
            mixed = mixed * here + mixed_ref[:, span] * there
            total = total * here + total_ref[:, span] * there
            mixed = (mixed / total).astype(BF16)
            own_ref[:, span] = mixed[:rows]
            out_ref[:, span] = mixed[rows:]

        attend_part(logit_ref, query_own_ref, query_in_ref, keys, key_t, value, put)


def attend_rest(phase, logit, query_own, query_in, parts, keys):
    shape = jax.ShapeDtypeStruct(query_own.shape, BF16)
    n, both = keys[0].shape
    count = n * len(keys)
    return pl.pallas_call(
        attend_rest_kernel,
        out_shape=(shape, shape, TOKEN),
        in_specs=[SMEM, SMEM] + [VMEM] * (5 + len(keys)),
        out_specs=(VMEM, VMEM, VMEM),
        scratch_shapes=[pltpu.VMEM((both, count), BF16), pltpu.VMEM((count, both), BF16)],
        compiler_params=params(28),
        cost_estimate=cost(6 * 10**10, 4 * 10**6),
        name="attend_rest",
    )(phase.reshape(1), logit, query_own, query_in, *parts, *keys)


def exit_kernel(phase_ref, core_ref, rows_ref, own_ref, in_ref, exit_ref, out_ref, token_ref):
    token_ref[...] = jnp.zeros_like(token_ref)
    n = own_ref.shape[0]
    on = phase_ref[0] == 1

    @pl.when(on)
    def _():
        attended = jnp.concatenate([own_ref[...], in_ref[...]], axis=0)
        mixed = dot(attended, exit_ref[...])
        for i in range(2):
            owner = core_ref[0] if i == 0 else 1 - core_ref[0]
            span = pl.ds(pl.multiple_of(owner * n, n), n)
            out_ref[span, :] = (rows_ref[span, :].astype(F32) + mixed[i * n : (i + 1) * n]).astype(
                BF16
            )

    @pl.when(jnp.logical_not(on))
    def _():
        out_ref[...] = rows_ref[...]


def leave(phase, core, encoded, own, arrived, exit_projector):
    return pl.pallas_call(
        exit_kernel,
        out_shape=(jax.ShapeDtypeStruct(encoded.shape, BF16), TOKEN),
        in_specs=[SMEM, SMEM] + [VMEM] * 4,
        out_specs=(VMEM, VMEM),
        compiler_params=params(32),
        cost_estimate=cost(8 * 10**8, 5 * 10**6),
        name="leave",
    )(phase.reshape(1), core.reshape(1), encoded, own, arrived, exit_projector)


def gather_terms_kernel(pieces_ref, _, out_ref):
    embed = out_ref.shape[2]
    total = jnp.sum(pieces_ref[...].astype(F32), axis=0)
    for kind in range(2):
        out_ref[kind] = total[:, kind * embed : (kind + 1) * embed]


def sum_terms(pieces, after):
    _, rows, width = pieces.shape
    return pl.pallas_call(
        gather_terms_kernel,
        out_shape=jax.ShapeDtypeStruct((2, rows, width // 2), F32),
        in_specs=[VMEM, ANY],
        out_specs=VMEM,
        compiler_params=params(32),
        cost_estimate=cost(10**6, 3 * 10**6),
        name="sum_terms",
    )(pieces, after)


def stack_kernel(*refs):
    blocks, (out_ref, token_ref) = refs[:-2], refs[-2:]
    rows = blocks[0].shape[0]
    for i, block in enumerate(blocks):
        out_ref[i * rows : (i + 1) * rows, :] = block[...]
    token_ref[...] = jnp.zeros_like(token_ref)


def stack(blocks):
    rows, width = blocks[0].shape
    return pl.pallas_call(
        stack_kernel,
        out_shape=(jax.ShapeDtypeStruct((len(blocks) * rows, width), BF16), TOKEN),
        in_specs=[VMEM] * len(blocks),
        out_specs=(VMEM, VMEM),
        compiler_params=params(8),
        cost_estimate=cost(10**5, 10**6),
        name="stack",
    )(*blocks)


def line_pairs(side, first, distance):
    pairs = []
    for y in range(side):
        for x in range(side):
            for core in range(2):
                along_x = (core == 0) == first
                to_x = (x + distance) % side if along_x else x
                to_y = y if along_x else (y + distance) % side
                pairs.append(((y * side + x) * 2 + core, (to_y * side + to_x) * 2 + core))
    return pairs


def lines_of(side, first, depth):
    groups = []
    for i in range(side):
        for core in range(2):
            along_x = (core == 0) == first
            chips = [i * side + k if along_x else k * side + i for k in range(side)]
            groups.append([(chip * 2 + core) * depth + d for chip in chips for d in range(depth)])
    return groups


def spread(block, side, first, order):
    return [lax.ppermute(block, SEQ, line_pairs(side, first, k)) for k in order]


def halo(first, last):
    count = lax.axis_size(SEQ)
    forward = [(i, i + 1) for i in range(count - 1)]
    backward = [(b, a) for a, b in forward]
    return lax.ppermute(last, SEQ, forward), lax.ppermute(first, SEQ, backward)


def body(
    bin_activations,
    spaced_filter_coefs,
    merged_bin_projector,
    backbone_rms_gain,
    asking_projector,
    common_lookup_projector,
    attention_exit_projector,
    lane_logit_factor,
    splice_readout_lines,
    couple_embedding_cotangent,
    splice_site_projector,
    site_locator_code,
    site_local_line,
    filled_slot_totals,
):
    phase = lax.axis_index("phase")
    core = lax.axis_index("core")
    batch, cells, chans = bin_activations.shape
    rows = cells // 2
    width = merged_bin_projector.shape[1]
    extent = DILATION_STEP * (spaced_filter_coefs.shape[0] // 2)
    lane = common_lookup_projector.shape[1] // 2
    shards = site_locator_code.shape[3]
    swap = [(0, 1), (1, 0)]
    side = lax.axis_size("y")

    first, last = bin_activations[:, :extent], bin_activations[:, -extent:]
    low, high = halo(first, last)
    payload, picked = pick(
        jnp.swapaxes(site_locator_code[0, :, 0], 1, 2),
        jnp.swapaxes(site_local_line[0, :, 0], 1, 2),
        filled_slot_totals[0, :, 0],
        couple_embedding_cotangent[0],
    )
    payload = follow(payload, low, high)
    arrived = lax.all_to_all(payload, SEQ, 0, 0, tiled=True)

    encoded, key_own, key_out, query_own, query_out, _ = encode(
        core,
        bin_activations,
        low,
        high,
        backbone_rms_gain,
        spaced_filter_coefs,
        merged_bin_projector,
        common_lookup_projector,
        asking_projector,
        picked,
    )
    chip_keys, chip_done = stack([key_own, lax.ppermute(key_out, "core", swap)])
    line_keys, line_done = stack([chip_keys] + spread(chip_keys, side, True, (2, 1, side - 1)))
    keys = [line_keys] + spread(line_keys, side, False, (1, side - 1, 2))
    query_in = lax.ppermute(query_out, "core", swap)

    portion = splice_readout_lines[0].reshape(batch * rows, width)
    place = jnp.stack([core, lax.axis_index("y"), lax.axis_index("x")]).astype(I32)
    mine, other = turn(place, portion, shards // 2, chip_done)
    other = lax.ppermute(other, "core", swap)

    ends = make_ends(arrived, batch, rows, line_done, other)
    ends_other = lax.ppermute(ends, "core", swap)
    *partial, terms_done = partial_grad(mine, other, ends, ends_other, side)
    terms = [partial[0]] + [
        lax.ppermute(partial[k], SEQ, line_pairs(side, True, k)) for k in (1, side - 1, 2)
    ]

    row_grad = make_row_grad(ends, splice_site_projector, terms_done)
    row_grad = row_grad.reshape(batch, rows, width)[None]

    logit = lane_logit_factor * (math.log2(math.e) / math.sqrt(lane))
    parts = attend_first(phase, logit, query_own, query_in, keys[:2], terms_done)
    own, out, attended = attend_rest(phase, logit, query_own, query_in, parts, keys[2:])
    rows_out, left = leave(
        phase, core, encoded, own, lax.ppermute(out, "core", swap), attention_exit_projector
    )
    phase_rows = rows_out.reshape(batch, rows, width)[None]

    depth = lax.axis_size("dp")
    line_terms = line_sum(terms, side * depth, attended)
    pieces = lax.all_to_all(
        line_terms,
        SEQ + ("dp",),
        0,
        0,
        axis_index_groups=lines_of(side, False, depth),
        tiled=True,
    )
    weight_grad = sum_terms(pieces, left)[None]
    return (phase_rows, row_grad, weight_grad)


def solution(mesh):
    shape = dict(mesh.shape)
    side = math.isqrt(shape["seq"] // 2)
    fine = Mesh(
        mesh.devices.reshape(shape["phase"], side, side, 2, shape["dp"]),
        ("phase", "y", "x", "core", "dp"),
    )
    return jax.shard_map(
        body,
        mesh=fine,
        in_specs=(
            P("dp", SEQ, None),
            P(),
            P(),
            P(),
            P(),
            P(),
            P(),
            P(),
            P("phase", "dp", SEQ, None),
            P("phase", "dp", SEQ, None),
            P(),
            P("phase", "dp", SEQ, None, None),
            P("phase", "dp", SEQ, None, None),
            P("phase", "dp", SEQ, None),
        ),
        out_specs=(
            P("phase", "dp", SEQ, None),
            P("phase", "dp", SEQ, None),
            P("phase", None, SEQ + ("dp",), None),
        ),
        check_vma=False,
    )
```

```python
import functools
import math

import jax
import jax.numpy as jnp
from jax import lax
from jax.experimental import pallas as pl
from jax.experimental.pallas import tpu as pltpu
from jax.sharding import Mesh
from jax.sharding import PartitionSpec as P

DILATION_STEP = 2
SEQ = ("y", "x", "core")
F32 = jnp.float32
BF16 = jnp.bfloat16
I32 = jnp.int32
TAG = 128
NT = (((1,), (1,)), ((), ()))
TN = (((0,), (0,)), ((), ()))
VMEM = pl.BlockSpec(memory_space=pltpu.VMEM)
SMEM = pl.BlockSpec(memory_space=pltpu.SMEM)
ANY = pl.BlockSpec(memory_space=pl.ANY)
HBM = pl.BlockSpec(memory_space=pltpu.HBM)


def dot(a, b, dims=(((1,), (0,)), ((), ()))):
    return lax.dot_general(a, b, dims, preferred_element_type=F32)


def params(mib):
    return pltpu.CompilerParams(vmem_limit_bytes=mib << 20)


TOKEN = jax.ShapeDtypeStruct((8, 128), F32)


def cost(flops, nbytes):
    return pl.CostEstimate(flops=int(flops), bytes_accessed=int(nbytes), transcendentals=0)


def pick_kernel(
    ids_hbm,
    lines_hbm,
    counts_hbm,
    cot_hbm,
    out_ref,
    token_ref,
    ids_ref,
    lines_ref,
    counts_ref,
    cot_ref,
    sems,
):
    pairs = ((ids_hbm, ids_ref), (lines_hbm, lines_ref), (counts_hbm, counts_ref), (cot_hbm, cot_ref))
    copies = [
        pltpu.make_async_copy(source, target, sems.at[i])
        for i, (source, target) in enumerate(pairs)
    ]
    for copy in copies:
        copy.start()
    token_ref[...] = jnp.zeros_like(token_ref)
    batch, slots, shards = ids_ref.shape
    junc, embed = cot_ref.shape[1:]
    n = shards * slots
    owner = lax.broadcasted_iota(I32, (n, shards), 0) // slots
    spread = owner == lax.broadcasted_iota(I32, (n, shards), 1)
    spread16 = spread.astype(F32).astype(BF16)
    slot = lax.broadcasted_iota(I32, (n, slots), 0) % slots
    own = slot == lax.broadcasted_iota(I32, (n, slots), 1)

    def column(values):
        wide = dot(spread16, values.astype(F32).astype(BF16), NT)
        return jnp.sum(jnp.where(own, wide, 0.0), axis=1, keepdims=True)

    for copy in copies:
        copy.wait()
    tags = []
    for b in range(batch):
        ids = ids_ref[b]
        junction = column(ids % junc)
        code = column(ids // junc) * float(junc) + column(lines_ref[b])
        count = jnp.sum(
            jnp.where(spread, counts_ref[b : b + 1, :].astype(F32), 0.0), axis=1, keepdims=True
        )
        valid = slot[:, :1].astype(F32) < count
        junction = jnp.where(valid, junction, -1.0).astype(I32)
        tags.append(jnp.broadcast_to(jnp.where(valid, code, -1.0), (n, TAG)))
        onehot = (junction == lax.broadcasted_iota(I32, (n, junc), 1)).astype(F32).astype(BF16)
        picked = dot(onehot, cot_ref[b]).astype(BF16)
        out_ref[:, :, b * embed : (b + 1) * embed] = picked.reshape(shards, slots, embed)
    lane = lax.broadcasted_iota(I32, (n, TAG), 1)
    tag = tags[0]
    for b in range(1, batch):
        tag = jnp.where(lane < b * (TAG // batch), tag, tags[b])
    out_ref[:, :, batch * embed :] = tag.astype(BF16).reshape(shards, slots, TAG)


def pick(ids, lines, counts, cotangent):
    batch, slots, shards = ids.shape
    embed = cotangent.shape[2]
    return pl.pallas_call(
        pick_kernel,
        out_shape=(
            jax.ShapeDtypeStruct((shards, slots, batch * embed + TAG), BF16),
            TOKEN,
        ),
        in_specs=[ANY] * 4,
        out_specs=(VMEM, VMEM),
        scratch_shapes=[
            pltpu.VMEM(ids.shape, I32),
            pltpu.VMEM(lines.shape, I32),
            pltpu.VMEM(counts.shape, I32),
            pltpu.VMEM(cotangent.shape, BF16),
            pltpu.SemaphoreType.DMA((4,)),
        ],
        compiler_params=params(56),
        cost_estimate=cost(2 * 10**8, 3 * 10**6),
        name="pick",
    )(ids, lines, counts, cotangent)


def follow(value, *after):
    return pl.pallas_call(
        lambda *refs: None,
        out_shape=jax.ShapeDtypeStruct(value.shape, value.dtype),
        in_specs=[ANY] * (1 + len(after)),
        out_specs=ANY,
        input_output_aliases={0: 0},
        name="follow",
    )(value, *after)


def ends_kernel(arrived_ref, _token, _other, out_ref):
    shards, slots, wide = arrived_ref.shape
    embed = out_ref.shape[1] // 2
    batch = (wide - TAG) // embed
    n = shards * slots
    rows = out_ref.shape[0] // batch
    tags = arrived_ref[:, :, batch * embed :].reshape(n, TAG).astype(F32)
    for b in range(batch):
        data = arrived_ref[:, :, b * embed : (b + 1) * embed].reshape(n, embed)
        lane = b * (TAG // batch)
        tag = jnp.broadcast_to(tags[:, lane : lane + 1], (n, rows))
        for kind in range(2):
            target = lax.broadcasted_iota(I32, (n, rows), 1) + kind * rows
            onehot = (tag == target.astype(F32)).astype(F32).astype(BF16)
            out_ref[b * rows : (b + 1) * rows, kind * embed : (kind + 1) * embed] = dot(
                onehot, data, TN
            ).astype(BF16)


def make_ends(arrived, batch, rows, token, other):
    embed = (arrived.shape[2] - TAG) // batch
    return pl.pallas_call(
        ends_kernel,
        out_shape=jax.ShapeDtypeStruct((batch * rows, 2 * embed), BF16),
        in_specs=[VMEM, ANY, ANY],
        out_specs=VMEM,
        compiler_params=params(14),
        cost_estimate=cost(4 * 10**8, 3 * 10**6),
        name="ends",
    )(arrived, token, other)


def row_grad_kernel(ends_ref, head_ref, _token, out_ref):
    embed = head_ref.shape[2]
    total = dot(ends_ref[:, :embed], head_ref[0], NT)
    total = total + dot(ends_ref[:, embed:], head_ref[1], NT)
    out_ref[...] = total.astype(BF16)


def make_row_grad(ends, head, token):
    n, both = ends.shape
    width, embed = head.shape[1:]
    step = 512
    return pl.pallas_call(
        row_grad_kernel,
        grid=(width // step,),
        out_shape=jax.ShapeDtypeStruct((n, width), BF16),
        in_specs=[
            pl.BlockSpec((n, both), lambda i: (0, 0)),
            pl.BlockSpec((2, step, embed), lambda i: (0, i, 0)),
            ANY,
        ],
        out_specs=pl.BlockSpec((n, step), lambda i: (0, i)),
        compiler_params=params(16),
        cost_estimate=cost(1.2 * 10**9, 6 * 10**6),
        name="row_grad",
    )(ends, head, token)


def turn_kernel(place_ref, lines_ref, _token, mine_ref, other_ref, turned):
    core, spot_y, spot_x = place_ref[0], place_ref[1], place_ref[2]
    blocks, part, n = mine_ref.shape
    side = math.isqrt(blocks)
    turned[...] = lines_ref[...].T.reshape(turned.shape)

    def block(core, k, i):
        on_x = i * side + lax.rem(spot_x + k, side)
        on_y = lax.rem(spot_y + k, side) * side + i
        return 2 * jnp.where(core == 0, on_x, on_y) + core

    for k in range(side):
        for i in range(side):
            mine_ref[k * side + i] = turned[block(core, k, i)]
            other_ref[k * side + i] = turned[block(1 - core, k, i)]


def turn(place, lines, blocks, after):
    n, width = lines.shape
    part = width // (2 * blocks)
    half = jax.ShapeDtypeStruct((blocks, part, n), BF16)
    return pl.pallas_call(
        turn_kernel,
        out_shape=(half, half),
        in_specs=[SMEM, VMEM, ANY],
        out_specs=(VMEM, VMEM),
        scratch_shapes=[pltpu.VMEM((2 * blocks, part, n), BF16)],
        compiler_params=params(10),
        cost_estimate=cost(10**6, 2 * 10**6),
        name="turn",
    )(place, lines, after)


def partial_kernel(mine_ref, other_ref, ends_ref, ends_other_ref, *out_refs):
    token_ref = out_refs[-1]
    token_ref[...] = jnp.zeros_like(token_ref)
    n = mine_ref.shape[2]
    count = len(out_refs) - 1
    step = mine_ref.shape[0] // count
    for i, out_ref in enumerate(out_refs[:-1]):
        rows = out_ref.shape[0]
        span = slice(i * step, (i + 1) * step)
        total = dot(mine_ref[span].reshape(rows, n), ends_ref[...])
        total = total + dot(other_ref[span].reshape(rows, n), ends_other_ref[...])
        out_ref[...] = total.astype(BF16)


def partial_grad(mine, other, ends, ends_other, side):
    rows, width = mine.shape[0] * mine.shape[1], ends.shape[1]
    piece = jax.ShapeDtypeStruct((rows // side, width), BF16)
    return pl.pallas_call(
        partial_kernel,
        out_shape=(piece,) * side + (TOKEN,),
        in_specs=[VMEM] * 4,
        out_specs=(VMEM,) * (side + 1),
        compiler_params=params(14),
        cost_estimate=cost(1.2 * 10**9, 5 * 10**6),
        name="partial_grad",
    )(mine, other, ends, ends_other)


def line_sum_kernel(*refs):
    pieces, out_ref = refs[:-2], refs[-1]
    total = functools.reduce(jnp.add, [piece[...].astype(F32) for piece in pieces])
    out_ref[...] = total.astype(BF16).reshape(out_ref.shape)


def line_sum(pieces, count, after):
    rows, width = pieces[0].shape
    return pl.pallas_call(
        line_sum_kernel,
        out_shape=jax.ShapeDtypeStruct((count, rows // count, width), BF16),
        in_specs=[VMEM] * len(pieces) + [ANY],
        out_specs=VMEM,
        compiler_params=params(14),
        cost_estimate=cost(10**6, 3 * 10**6),
        name="line_sum",
    )(*pieces, after)


def encoder_kernel(
    core_ref,
    low_ref,
    high_ref,
    gain_ref,
    x_hbm,
    taps_hbm,
    merge_hbm,
    look_hbm,
    ask_hbm,
    after_ref,
    rows_hbm,
    key_own_ref,
    key_out_ref,
    query_own_ref,
    query_out_ref,
    token_ref,
    x_ref,
    taps,
    merge,
    look,
    ask,
    pad,
    hidden,
    rows_ref,
    sems,
):
    pairs = ((x_hbm, x_ref), (taps_hbm, taps), (merge_hbm, merge), (look_hbm, look), (ask_hbm, ask))
    copies = [
        pltpu.make_async_copy(source, target, sems.at[i])
        for i, (source, target) in enumerate(pairs)
    ]
    for copy in copies:
        copy.start()
    out_copy = pltpu.make_async_copy(rows_ref, rows_hbm, sems.at[len(pairs)])
    batch, cells, chans = x_ref.shape
    extent = low_ref.shape[1]
    base = 8
    copies[0].wait()
    for b in range(batch):
        pad[b, base - extent : base, :] = low_ref[b].astype(F32)
        pad[b, base : base + cells, :] = x_ref[b].astype(F32)
        pad[b, base + cells : base + cells + extent, :] = high_ref[b].astype(F32)
    copies[1].wait()
    for b in range(batch):
        before = pad[b, base - extent : base - extent + cells, :].astype(BF16)
        behind = pad[b, base + extent : base + extent + cells, :].astype(BF16)
        for j in range(0, chans, 256):
            span = slice(j, j + 256)
            total = dot(x_ref[b], taps[1, :, span])
            total += dot(before, taps[0, :, span]) + dot(behind, taps[2, :, span])
            total = pad[b, base : base + cells, span] + jax.nn.gelu(total)
            for i in range(0, 256, 128):
                hidden[(j + i) // 128, b * cells : (b + 1) * cells, :] = total[:, i : i + 128]
    n = batch * cells // 2
    pooled = jnp.concatenate(
        [
            ((hidden[j, pl.ds(0, n, 2), :] + hidden[j, pl.ds(1, n, 2), :]) * 0.5).astype(BF16)
            for j in range(hidden.shape[0])
        ],
        axis=1,
    )
    copies[2].wait()
    rows = dot(pooled, merge[...]).astype(BF16)
    rows_ref[...] = rows
    out_copy.start()
    wide = rows.astype(F32)
    scale = lax.rsqrt(jnp.mean(wide * wide, axis=-1, keepdims=True) + 1e-06)
    normed = (wide * scale * gain_ref[...]).astype(BF16)
    half = n // 2
    first = core_ref[0] == 0

    def halves(value, own_ref, out_ref):
        own_ref[...] = jnp.where(first, value[:half], value[half:])
        out_ref[...] = jnp.where(first, value[half:], value[:half])

    copies[3].wait()
    halves(dot(normed, look[...]).astype(BF16), key_own_ref, key_out_ref)
    copies[4].wait()
    halves(dot(normed, ask[...]).astype(BF16), query_own_ref, query_out_ref)
    token_ref[...] = jnp.zeros_like(token_ref)
    out_copy.wait()


def encode(core, x, low, high, gain, taps, merge, look, ask, after):
    batch, cells, chans = x.shape
    n = batch * cells // 2
    width = merge.shape[1]
    key = jax.ShapeDtypeStruct((n // 2, look.shape[1]), BF16)
    query = jax.ShapeDtypeStruct((n // 2, ask.shape[1]), BF16)
    return pl.pallas_call(
        encoder_kernel,
        out_shape=(jax.ShapeDtypeStruct((n, width), BF16), key, key, query, query, TOKEN),
        in_specs=[SMEM] + [VMEM] * 3 + [HBM] * 5 + [ANY],
        out_specs=(HBM,) + (VMEM,) * 5,
        scratch_shapes=[
            pltpu.VMEM(x.shape, BF16),
            pltpu.VMEM(taps.shape, BF16),
            pltpu.VMEM(merge.shape, BF16),
            pltpu.VMEM(look.shape, BF16),
            pltpu.VMEM(ask.shape, BF16),
            pltpu.VMEM((batch, cells + 16, chans), F32),
            pltpu.VMEM((chans // 128, batch * cells, 128), F32),
            pltpu.VMEM((n, width), BF16),
            pltpu.SemaphoreType.DMA((6,)),
        ],
        compiler_params=params(56),
        cost_estimate=cost(3.4 * 10**9, 12 * 10**6),
        name="encode",
    )(core.reshape(1), low, high, gain.reshape(1, width), x, taps, merge, look, ask, after)


def attend_part(logit_ref, query_own_ref, query_in_ref, keys, key_t, value, put):
    rows, width = query_own_ref.shape
    n, both = keys[0].shape
    lane = both // 2
    count = n * len(keys)
    chunk = 512
    for i, block in enumerate(keys):
        span = slice(i * n, (i + 1) * n)
        turned = block[:, :lane].T
        key_t[:lane, span] = turned
        key_t[lane:, span] = turned
        value[span, :lane] = block[:, lane:]
        value[span, lane:] = jnp.ones((n, lane), BF16)
    for head in range(width // lane):
        span = slice(head * lane, (head + 1) * lane)
        query = jnp.concatenate([query_own_ref[:, span], query_in_ref[:, span]], axis=0)
        query = query.astype(F32) * logit_ref[head]
        coarse = query.astype(BF16)
        fine = (query - coarse.astype(F32)).astype(BF16)
        query = jnp.concatenate([coarse, fine], axis=1)
        scores = [dot(query, key_t[:, j : j + chunk]) for j in range(0, count, chunk)]
        top = jnp.max(functools.reduce(jnp.maximum, scores), axis=-1, keepdims=True)
        mixed = 0.0
        for j, score in enumerate(scores):
            weight = jnp.exp2(score - top).astype(BF16)
            mixed = mixed + dot(weight, value[j * chunk : (j + 1) * chunk, :])
        put(span, mixed[:, :lane], mixed[:, lane:], jnp.broadcast_to(top, (2 * rows, lane)))


def attend_first_kernel(phase_ref, logit_ref, query_own_ref, query_in_ref, *refs):
    keys, (_, mixed_ref, total_ref, top_ref, key_t, value) = refs[:-6], refs[-6:]

    @pl.when(phase_ref[0] == 1)
    def _():
        def put(span, mixed, total, top):
            mixed_ref[:, span] = mixed
            total_ref[:, span] = total
            top_ref[:, span] = top

        attend_part(logit_ref, query_own_ref, query_in_ref, keys, key_t, value, put)


def attend_first(phase, logit, query_own, query_in, keys, after):
    n, both = keys[0].shape
    count = n * len(keys)
    rows, width = query_own.shape
    part = jax.ShapeDtypeStruct((2 * rows, width), F32)
    return pl.pallas_call(
        attend_first_kernel,
        out_shape=(part, part, part),
        in_specs=[SMEM, SMEM] + [VMEM] * (2 + len(keys)) + [ANY],
        out_specs=(VMEM,) * 3,
        scratch_shapes=[pltpu.VMEM((both, count), BF16), pltpu.VMEM((count, both), BF16)],
        compiler_params=params(28),
        cost_estimate=cost(10**9, 4 * 10**6),
        name="attend_first",
    )(phase.reshape(1), logit, query_own, query_in, *keys, after)


def attend_rest_kernel(
    phase_ref, logit_ref, query_own_ref, query_in_ref, mixed_ref, total_ref, top_ref, *refs
):
    keys, (own_ref, out_ref, token_ref, key_t, value) = refs[:-5], refs[-5:]
    token_ref[...] = jnp.zeros_like(token_ref)
    rows = query_own_ref.shape[0]

    @pl.when(phase_ref[0] == 1)
    def _():
        def put(span, mixed, total, top):
            highest = jnp.maximum(top, top_ref[:, span])
            here, there = jnp.exp2(top - highest), jnp.exp2(top_ref[:, span] - highest)
            mixed = mixed * here + mixed_ref[:, span] * there
            total = total * here + total_ref[:, span] * there
            mixed = (mixed / total).astype(BF16)
            own_ref[:, span] = mixed[:rows]
            out_ref[:, span] = mixed[rows:]

        attend_part(logit_ref, query_own_ref, query_in_ref, keys, key_t, value, put)


def attend_rest(phase, logit, query_own, query_in, parts, keys):
    shape = jax.ShapeDtypeStruct(query_own.shape, BF16)
    n, both = keys[0].shape
    count = n * len(keys)
    return pl.pallas_call(
        attend_rest_kernel,
        out_shape=(shape, shape, TOKEN),
        in_specs=[SMEM, SMEM] + [VMEM] * (5 + len(keys)),
        out_specs=(VMEM, VMEM, VMEM),
        scratch_shapes=[pltpu.VMEM((both, count), BF16), pltpu.VMEM((count, both), BF16)],
        compiler_params=params(28),
        cost_estimate=cost(6 * 10**10, 4 * 10**6),
        name="attend_rest",
    )(phase.reshape(1), logit, query_own, query_in, *parts, *keys)


def exit_kernel(phase_ref, core_ref, rows_ref, own_ref, in_ref, exit_ref, out_ref, token_ref):
    token_ref[...] = jnp.zeros_like(token_ref)
    n = own_ref.shape[0]
    on = phase_ref[0] == 1

    @pl.when(on)
    def _():
        attended = jnp.concatenate([own_ref[...], in_ref[...]], axis=0)
        mixed = dot(attended, exit_ref[...])
        for i in range(2):
            owner = core_ref[0] if i == 0 else 1 - core_ref[0]
            span = pl.ds(pl.multiple_of(owner * n, n), n)
            out_ref[span, :] = (rows_ref[span, :].astype(F32) + mixed[i * n : (i + 1) * n]).astype(
                BF16
            )

    @pl.when(jnp.logical_not(on))
    def _():
        out_ref[...] = rows_ref[...]


def leave(phase, core, encoded, own, arrived, exit_projector):
    return pl.pallas_call(
        exit_kernel,
        out_shape=(jax.ShapeDtypeStruct(encoded.shape, BF16), TOKEN),
        in_specs=[SMEM, SMEM] + [VMEM] * 4,
        out_specs=(VMEM, VMEM),
        compiler_params=params(14),
        cost_estimate=cost(8 * 10**8, 5 * 10**6),
        name="leave",
    )(phase.reshape(1), core.reshape(1), encoded, own, arrived, exit_projector)


def gather_terms_kernel(pieces_ref, _, out_ref):
    embed = out_ref.shape[2]
    total = jnp.sum(pieces_ref[...].astype(F32), axis=0)
    for kind in range(2):
        out_ref[kind] = total[:, kind * embed : (kind + 1) * embed]


def sum_terms(pieces, after):
    _, rows, width = pieces.shape
    return pl.pallas_call(
        gather_terms_kernel,
        out_shape=jax.ShapeDtypeStruct((2, rows, width // 2), F32),
        in_specs=[VMEM, ANY],
        out_specs=VMEM,
        compiler_params=params(10),
        cost_estimate=cost(10**6, 3 * 10**6),
        name="sum_terms",
    )(pieces, after)


def stack_kernel(*refs):
    blocks, (out_ref, token_ref) = refs[:-2], refs[-2:]
    rows = blocks[0].shape[0]
    for i, block in enumerate(blocks):
        out_ref[i * rows : (i + 1) * rows, :] = block[...]
    token_ref[...] = jnp.zeros_like(token_ref)


def stack(blocks):
    rows, width = blocks[0].shape
    return pl.pallas_call(
        stack_kernel,
        out_shape=(jax.ShapeDtypeStruct((len(blocks) * rows, width), BF16), TOKEN),
        in_specs=[VMEM] * len(blocks),
        out_specs=(VMEM, VMEM),
        compiler_params=params(8),
        cost_estimate=cost(10**5, 10**6),
        name="stack",
    )(*blocks)


def line_pairs(side, first, distance):
    pairs = []
    for y in range(side):
        for x in range(side):
            for core in range(2):
                along_x = (core == 0) == first
                to_x = (x + distance) % side if along_x else x
                to_y = y if along_x else (y + distance) % side
                pairs.append(((y * side + x) * 2 + core, (to_y * side + to_x) * 2 + core))
    return pairs


def lines_of(side, first, depth):
    groups = []
    for i in range(side):
        for core in range(2):
            along_x = (core == 0) == first
            chips = [i * side + k if along_x else k * side + i for k in range(side)]
            groups.append([(chip * 2 + core) * depth + d for chip in chips for d in range(depth)])
    return groups


def spread(block, side, first, order):
    return [lax.ppermute(block, SEQ, line_pairs(side, first, k)) for k in order]


def halo(first, last):
    count = lax.axis_size(SEQ)
    forward = [(i, i + 1) for i in range(count - 1)]
    backward = [(b, a) for a, b in forward]
    return lax.ppermute(last, SEQ, forward), lax.ppermute(first, SEQ, backward)


def body(
    bin_activations,
    spaced_filter_coefs,
    merged_bin_projector,
    backbone_rms_gain,
    asking_projector,
    common_lookup_projector,
    attention_exit_projector,
    lane_logit_factor,
    splice_readout_lines,
    couple_embedding_cotangent,
    splice_site_projector,
    site_locator_code,
    site_local_line,
    filled_slot_totals,
):
    phase = lax.axis_index("phase")
    core = lax.axis_index("core")
    batch, cells, chans = bin_activations.shape
    rows = cells // 2
    width = merged_bin_projector.shape[1]
    extent = DILATION_STEP * (spaced_filter_coefs.shape[0] // 2)
    lane = common_lookup_projector.shape[1] // 2
    shards = site_locator_code.shape[3]
    swap = [(0, 1), (1, 0)]
    side = lax.axis_size("y")

    first, last = bin_activations[:, :extent], bin_activations[:, -extent:]
    low, high = halo(first, last)
    payload, picked = pick(
        jnp.swapaxes(site_locator_code[0, :, 0], 1, 2),
        jnp.swapaxes(site_local_line[0, :, 0], 1, 2),
        filled_slot_totals[0, :, 0],
        couple_embedding_cotangent[0],
    )
    payload = follow(payload, low, high)
    arrived = lax.all_to_all(payload, SEQ, 0, 0, tiled=True)

    encoded, key_own, key_out, query_own, query_out, _ = encode(
        core,
        bin_activations,
        low,
        high,
        backbone_rms_gain,
        spaced_filter_coefs,
        merged_bin_projector,
        common_lookup_projector,
        asking_projector,
        picked,
    )
    chip_keys, chip_done = stack([key_own, lax.ppermute(key_out, "core", swap)])
    line_keys, line_done = stack([chip_keys] + spread(chip_keys, side, True, (2, 1, side - 1)))
    keys = [line_keys] + spread(line_keys, side, False, (1, side - 1, 2))
    query_in = lax.ppermute(query_out, "core", swap)

    portion = splice_readout_lines[0].reshape(batch * rows, width)
    place = jnp.stack([core, lax.axis_index("y"), lax.axis_index("x")]).astype(I32)
    mine, other = turn(place, portion, shards // 2, chip_done)
    other = lax.ppermute(other, "core", swap)

    ends = make_ends(arrived, batch, rows, line_done, other)
    ends_other = lax.ppermute(ends, "core", swap)
    *partial, terms_done = partial_grad(mine, other, ends, ends_other, side)
    terms = [partial[0]] + [
        lax.ppermute(partial[k], SEQ, line_pairs(side, True, k)) for k in (1, side - 1, 2)
    ]

    row_grad = make_row_grad(ends, splice_site_projector, terms_done)
    row_grad = row_grad.reshape(batch, rows, width)[None]

    logit = lane_logit_factor * (math.log2(math.e) / math.sqrt(lane))
    parts = attend_first(phase, logit, query_own, query_in, keys[:2], terms_done)
    own, out, attended = attend_rest(phase, logit, query_own, query_in, parts, keys[2:])
    rows_out, left = leave(
        phase, core, encoded, own, lax.ppermute(out, "core", swap), attention_exit_projector
    )
    phase_rows = rows_out.reshape(batch, rows, width)[None]

    depth = lax.axis_size("dp")
    line_terms = line_sum(terms, side * depth, attended)
    pieces = lax.all_to_all(
        line_terms,
        SEQ + ("dp",),
        0,
        0,
        axis_index_groups=lines_of(side, False, depth),
        tiled=True,
    )
    weight_grad = sum_terms(pieces, left)[None]
    return (phase_rows, row_grad, weight_grad)


def solution(mesh):
    shape = dict(mesh.shape)
    side = math.isqrt(shape["seq"] // 2)
    fine = Mesh(
        mesh.devices.reshape(shape["phase"], side, side, 2, shape["dp"]),
        ("phase", "y", "x", "core", "dp"),
    )
    return jax.shard_map(
        body,
        mesh=fine,
        in_specs=(
            P("dp", SEQ, None),
            P(),
            P(),
            P(),
            P(),
            P(),
            P(),
            P(),
            P("phase", "dp", SEQ, None),
            P("phase", "dp", SEQ, None),
            P(),
            P("phase", "dp", SEQ, None, None),
            P("phase", "dp", SEQ, None, None),
            P("phase", "dp", SEQ, None),
        ),
        out_specs=(
            P("phase", "dp", SEQ, None),
            P("phase", "dp", SEQ, None),
            P("phase", None, SEQ + ("dp",), None),
        ),
        check_vma=False,
    )
```
